128 devices in a mesh: intra: 8 (over y, z_hi), inter: 16 (over z_lo, x, core).
Axes of the slice: x: 4, y: 4, z: 4 (z_hi: 2, z_lo: 2; z = z_hi * 2 + z_lo), core: 2. Of those that a mesh axis runs over, the one named last changes fastest.
Arguments:
- activations: bfloat16 [65536, 8192], P(('intra', 'inter')), may hold values from -24 to 24
- key_grads: bfloat16 [65536, 1024], P(('intra', 'inter')), may hold values from -6 to 6
- key_weight: bfloat16 [8192, 1024], P('intra'), may hold values from -0.1875 to 0.1875
Outputs:
- input_grads: bfloat16 [65536, 8192], P(('intra', 'inter'))
- weight_grads: float32 [8192, 1024], P(('intra', 'inter'))
The draws below stay inside these ranges and needn't reach their ends.
All inputs are finite; a program needn't handle non-finite values. Where the reference program divides by a largest or mean magnitude, that divisor is 1e-20 or more.
Results may differ from the reference program's by a relative error of at most 0.013.
Values may be sent and summed in bfloat16 or wider, within the bound.
No kernel may reach another device: no remote copies, remote signals or barrier semaphores. Data moves between devices by JAX's collectives and lax.ppermute only.
A program may use at most 256 MiB of HBM per device.

```python
import jax
import jax.numpy as jnp
from jax import lax

D = 8192
KV = 1024
TOK_DEV = 512
TOKENS = 65536
N_INTRA = 8
N_INTER = 16


def with_spikes(array, own_key, source, target, parts, factor):
    def block_of(dim):
        return (jnp.arange(array.shape[dim]) // (array.shape[dim] // parts)).reshape((-1,) + (1,) * (array.ndim - 1 - dim))

    near = jax.random.permutation(own_key, parts)[block_of(target)]
    far = (block_of(target) + parts // 2) % parts
    return jnp.where((block_of(source) == near) | (block_of(source) == far), factor * array, array)


def block_scale(own_key, extent, shards, low, high):
    def one(dim, blocks):
        draws = jax.random.uniform(jax.random.fold_in(jax.random.fold_in(own_key, 6), dim), (blocks,), jnp.float32, low / len(shards), high / len(shards))
        return jnp.repeat(jnp.exp(draws), extent[dim] // blocks).reshape((-1,) + (1,) * (len(extent) - dim - 1))

    gain = one(*shards[0])
    for cut in shards[1:]:
        gain = gain * one(*cut)
    return gain


def gaussian(stream_key, dims, width, limit, split=(), held_as=jnp.bfloat16):
    loudness = block_scale(stream_key, dims, split, -0.22, 0.18) if split else 1.0
    values = jax.random.normal(stream_key, dims, jnp.float32) * width * loudness
    return jnp.minimum(jnp.maximum(values, -limit), limit).astype(held_as)


def bell_draw_with(own_key, extent, width, bound, pieces, heavy, kind=jnp.bfloat16):
    drawn = width * jax.random.normal(own_key, extent, jnp.float32)
    if pieces:
        drawn = drawn * block_scale(own_key, extent, pieces, -0.22, 0.18)
    return jnp.clip(with_spikes(drawn, jax.random.fold_in(own_key, 3), *heavy), -bound, bound).astype(kind)


def setup_inputs(seed: int = 0) -> dict:
    arg_keys = jax.random.split(jax.random.key(seed), 4)
    return {
        "activations": bell_draw_with(arg_keys[0], (TOKENS, D), 1.0, 24.0, ((0, 128),), (0, 1, 128, 5.5)),
        "key_grads": gaussian(arg_keys[1], (TOKENS, KV), 1.0, 6.0, ((0, 128),)),
        "key_weight": gaussian(arg_keys[2], (D, KV), KV ** -0.5, 0.1875, ((0, 8),)),
    }


EPS = 1e-6


def dequantize(values):
    blocks = values.reshape(values.shape[0], KV // 128, 128)
    maxima = jnp.max(jnp.abs(blocks), axis=-1, keepdims=True) + EPS
    quantized = lax.optimization_barrier((blocks / maxima).astype(jnp.bfloat16))
    return quantized.astype(jnp.float32) * maxima


def reference(activations, key_grads, key_weight):
    norm_factor = TOKENS ** -0.5
    inputs_grid = activations.reshape(N_INTRA, N_INTER, TOK_DEV, D)
    grads_grid = key_grads.reshape(N_INTRA, N_INTER, TOK_DEV, KV)

    def node_step(running, node_index):
        def member(node_total, member_index):
            partial_value = jnp.dot(inputs_grid[member_index, node_index].T, grads_grid[member_index, node_index], preferred_element_type=jnp.float32) * norm_factor
            return node_total + dequantize(partial_value), None

        node_total, unused = lax.scan(member, jnp.zeros((D, KV // 128, 128), jnp.float32), jnp.arange(N_INTRA, dtype=jnp.int32))
        return running + dequantize(node_total.reshape(D, KV)), None

    running, unused = lax.scan(node_step, jnp.zeros((D, KV // 128, 128), jnp.float32), jnp.arange(N_INTER, dtype=jnp.int32))
    weight_grads = running.reshape(D, KV)

    def project(grad_block):
        return jnp.dot(grad_block, key_weight.T, preferred_element_type=jnp.float32).astype(jnp.bfloat16)

    input_grads = lax.map(project, key_grads.reshape(N_INTRA * N_INTER, TOK_DEV, KV)).reshape(TOKENS, D)
    return input_grads, weight_grads
```

```python
import functools

import jax
import jax.numpy as jnp
import numpy as np
from jax import lax
from jax.experimental import pallas as pl
from jax.experimental.pallas import tpu as pltpu
from jax.sharding import PartitionSpec as P

SIZES = (4, 2, 2, 4, 2)
AXES = ("intra", "inter")
S1 = 640
T1 = 336
BLK = 128

RS_A = ((("xA", "xB", "zD"), ("zD", "xA", "xB")), (("xB", "zD", "xA"), ("zD", "xA", "xB")))
RS_B = ((("zC", "yA"), ("yA", "zC")), (("yA", "zC"), ("zC", "yA")))
AG = ((("yA", "yB", "zC"), ("zC", "yA", "yB")), (("yB", "zC", "yA"), ("zC", "yA", "yB")))


def coords(device):
    return tuple(int(v) for v in np.unravel_index(device, SIZES))


def ident(at):
    return int(np.ravel_multi_index(at, SIZES))


def flip(at, dim):
    y, zh, zl, x, c = at
    return {
        "yA": (y ^ 1, zh, zl, x, c),
        "yB": (3 - y, zh, zl, x, c),
        "zC": (y, zh ^ 1, zl ^ 1, x, c),
        "zD": (y, zh, zl ^ 1, x, c),
        "xA": (y, zh, zl, x ^ 1, c),
        "xB": (y, zh, zl, 3 - x, c),
        "core": (y, zh, zl, x, 1 - c),
    }[dim]


def table():
    rows = []
    for device in range(128):
        at = coords(device)
        core = at[4]
        row = []
        for stream in range(2):
            dims = RS_A[core][stream] + RS_B[core][stream]
            for j in range(32):
                owner = at
                if (at[0] >> 1) != core:
                    owner = flip(owner, "yB")
                for k, dim in enumerate(dims):
                    if (j >> (4 - k)) & 1:
                        owner = flip(owner, dim)
                assert owner[0] >> 1 == core
                row.append(ident(owner) // 2 - 32 * core)
        for gatherer in (core, 1 - core):
            for stream in range(2):
                for j in range(8):
                    holder = at
                    for k, dim in enumerate(AG[gatherer][stream]):
                        if (j >> k) & 1:
                            holder = flip(holder, dim)
                    row.append(holder[0] * 2 + holder[1])
        rows.append(row)
    return np.array(rows, np.int32)


def move(value, dims_of_core):
    pairs = []
    for device in range(128):
        at = coords(device)
        pairs.append((device, ident(flip(at, dims_of_core[at[4]]))))
    return lax.ppermute(value, AXES, pairs)


def move_some(value, want_mine, dims):
    pairs = []
    for device in range(128):
        at = coords(device)
        if ((at[0] >> 1) == at[4]) == want_mine:
            to = at
            for dim in dims:
                to = flip(to, dim)
            pairs.append((device, ident(to)))
    return lax.ppermute(value, AXES, pairs)


def partial_body(low, high, norm, idx_ref, *refs):
    own = jnp.concatenate([ref[...] for ref in refs[0:4]], axis=1)
    got = jnp.concatenate([ref[...] for ref in refs[4:8]], axis=1)
    kt_own, kt_got, out_ref = refs[8:]
    total = jnp.dot(kt_own[low:high, :], own, preferred_element_type=jnp.float32)
    total += jnp.dot(kt_got[low:high, :], got, preferred_element_type=jnp.float32)
    total = (total * norm).astype(jnp.bfloat16)
    for k in range(4):
        out_ref[k] = total[:, k * BLK : (k + 1) * BLK]


def partial_blocks(idx, core, acts, acts_got, kt_own, kt_got, low, high, norm):
    tokens = acts.shape[0]
    count = idx.shape[0]
    where = jnp.concatenate([idx + 32 * core, idx])
    specs = [
        pl.BlockSpec((tokens, BLK), functools.partial(lambda k, i, w: (0, w[4 * i + k]), k))
        for k in range(4)
    ] + [
        pl.BlockSpec((tokens, BLK), functools.partial(lambda k, i, w: (0, w[count + 4 * i + k]), k))
        for k in range(4)
    ]
    specs += [pl.BlockSpec(kt_own.shape, lambda i, w: (0, 0))] * 2
    width = high - low
    return pl.pallas_call(
        functools.partial(partial_body, low, high, norm),
        grid_spec=pltpu.PrefetchScalarGridSpec(
            num_scalar_prefetch=1,
            grid=(count // 4,),
            in_specs=specs,
            out_specs=pl.BlockSpec((4, width, BLK), lambda i, w: (i, 0, 0)),
        ),
        out_shape=jax.ShapeDtypeStruct((count, width, BLK), jnp.bfloat16),
        compiler_params=pltpu.CompilerParams(vmem_limit_bytes=32 * 1024 * 1024),
        cost_estimate=pl.CostEstimate(
            flops=4 * tokens * width * count * BLK, bytes_accessed=count * BLK * (4 * tokens + 2 * width), transcendentals=0
        ),
    )(where, *([acts] * 4), *([acts_got] * 4), kt_own, kt_got)


def project_body(half, rest, sched_ref, kg_ref, *refs):
    pieces, out_ref, wbuf, sem_a, sem_b = refs[:8], refs[8], refs[9], refs[10], refs[11]
    step = pl.program_id(0)

    def piece(side, stream, j):
        source = pieces[side * 4 + stream * 2 + j // 4].at[j % 4]
        shard = sched_ref[16 + side * 16 + stream * 8 + j]
        rows = T1 if stream == 0 else rest
        first = shard * (2 * half) + sched_ref[48 + side] * half + (0 if stream == 0 else T1)
        sem = (sem_a if stream == 0 else sem_b).at[side * 8 + j]
        return pltpu.make_async_copy(source, wbuf.at[pl.ds(pl.multiple_of(first, 16), rows), :], sem)

    @pl.when(step == 0)
    def _():
        for side in range(2):
            for stream in (1, 0):
                for j in range(8):
                    piece(side, stream, j).start()

    for side in range(2):

        @pl.when(step == 8 * side)
        def _(side=side):
            for j in range(8):
                piece(side, 1, j).wait()

        for j in range(8):

            @pl.when(step == 8 * side + j)
            def _(side=side, j=j):
                piece(side, 0, j).wait()

    start = pl.multiple_of(sched_ref[step] * half, half)
    out_ref[...] = lax.dot_general(
        kg_ref[...], wbuf[pl.ds(start, half), :], (((1,), (1,)), ((), ())), preferred_element_type=jnp.float32
    ).astype(jnp.bfloat16)


def project(sched, key_grads, pieces, half):
    tokens, width = key_grads.shape
    rest = half - T1
    return pl.pallas_call(
        functools.partial(project_body, half, rest),
        grid_spec=pltpu.PrefetchScalarGridSpec(
            num_scalar_prefetch=1,
            grid=(16,),
            in_specs=[pl.BlockSpec((tokens, width), lambda i, s: (0, 0))] + [pl.BlockSpec(memory_space=pl.ANY)] * 8,
            out_specs=pl.BlockSpec((tokens, half), lambda i, s: (0, s[i])),
            scratch_shapes=[
                pltpu.VMEM((16 * half, width), jnp.bfloat16),
                pltpu.SemaphoreType.DMA((16,)),
                pltpu.SemaphoreType.DMA((16,)),
            ],
        ),
        out_shape=jax.ShapeDtypeStruct((tokens, 16 * half), jnp.bfloat16),
        compiler_params=pltpu.CompilerParams(vmem_limit_bytes=40 * 1024 * 1024),
        cost_estimate=pl.CostEstimate(
            flops=2 * tokens * width * 16 * half, bytes_accessed=2 * 16 * half * (width + tokens), transcendentals=0
        ),
    )(sched, key_grads, *pieces)


def add16(a, b):
    return (a.astype(jnp.float32) + b.astype(jnp.float32)).astype(jnp.bfloat16)


def shards(acts, key_grads, key_weight):
    tokens, model = acts.shape
    norm = float((tokens * 128) ** -0.5)
    device = lax.axis_index(AXES)
    core = device % 2
    y_hi = device // 64
    mine = core == y_hi
    row = lax.dynamic_index_in_dim(jnp.asarray(table()), device, 0, keepdims=False)

    to_other = lax.dynamic_slice_in_dim(acts, (1 - core) * (model // 2), model // 2, axis=1)
    acts_got = move(to_other, ("core", "core"))
    kt_own = key_grads.T
    kt_got = move(kt_own, ("core", "core"))

    half = key_weight.shape[0] // 2
    own_half = lax.dynamic_slice_in_dim(key_weight, core * half, half, axis=0)
    gathered = []
    for stream in range(2):
        have = (own_half[:T1] if stream == 0 else own_half[T1:])[None]
        for stage in range(2):
            got = move(have, (AG[0][stream][stage], AG[1][stream][stage]))
            have = jnp.concatenate([have, got], axis=0)
        got = move(have, (AG[0][stream][2], AG[1][stream][2]))
        gathered += [have, got]
    swapped = [move(g, ("core", "core")) for g in gathered]

    lows = (0, S1, key_grads.shape[1])
    part = functools.partial(partial_blocks, core=core, acts=acts, acts_got=acts_got, kt_own=kt_own, kt_got=kt_got, norm=norm)
    sends, keeps = [], []
    for stream in range(2):
        idx = row[32 * stream : 32 * stream + 32]
        sends.append(part(idx[16:], low=lows[stream], high=lows[stream + 1]))
    for stream in range(2):
        idx = row[32 * stream : 32 * stream + 32]
        keeps.append(part(idx[:16], low=lows[stream], high=lows[stream + 1]))
    finals = []
    for stream in range(2):
        dims = [RS_A[k][stream] + RS_B[k][stream] for k in range(2)]
        send, keep = sends[stream], keeps[stream]
        for stage in range(5):
            got = move(send, (dims[0][stage], dims[1][stage]))
            n = keep.shape[0] // 2
            if stage < 4:
                send, keep = add16(keep[n:], got[n:]), add16(keep[:n], got[:n])
            else:
                finals.append(keep[0].astype(jnp.float32) + got[0].astype(jnp.float32))

    total = jnp.concatenate(finals, axis=0).T
    rows = total.shape[0] // 2
    for_me = lax.dynamic_slice_in_dim(total, core * rows, rows, axis=0)
    for_other = lax.dynamic_slice_in_dim(total, (1 - core) * rows, rows, axis=0)
    for_me16, for_other16 = for_me.astype(jnp.bfloat16), for_other.astype(jnp.bfloat16)
    local = move_some(for_other, True, ("core",))
    same = move_some(for_me16, False, ("yB",))
    cross = move_some(for_other16, False, ("yB", "core"))
    weight_grads = jnp.where(mine, for_me, 0.0) + local + same.astype(jnp.float32) + cross.astype(jnp.float32)

    own, other = row[64:80], row[80:96]
    cores = jnp.stack([core, 1 - core]).astype(jnp.int32)
    order = jnp.concatenate([own[:8] * 2 + core, other[:8] * 2 + 1 - core])
    sched = jnp.concatenate([order, own, other, cores]).astype(jnp.int32)
    input_grads = project(sched, key_grads, gathered + swapped, half)
    return input_grads, weight_grads


def solution(mesh):
    spec = P(AXES, None)
    return jax.shard_map(
        shards, mesh=mesh, in_specs=(spec, spec, P("intra", None)), out_specs=(spec, spec), check_vma=False
    )
```

```python
import functools

import jax
import jax.numpy as jnp
import numpy as np
from jax import lax
from jax.experimental import pallas as pl
from jax.experimental.pallas import tpu as pltpu
from jax.sharding import PartitionSpec as P

SIZES = (4, 2, 2, 4, 2)
AXES = ("intra", "inter")
S1 = 640
T1 = 336
BLK = 128

RS_A = ((("xA", "xB", "zD"), ("zD", "xA", "xB")), (("xB", "zD", "xA"), ("zD", "xA", "xB")))
RS_B = ((("zC", "yA"), ("zC", "yA")), (("yA", "zC"), ("yA", "zC")))
AG = ((("yA", "yB", "zC"), ("zC", "yA", "yB")), (("yB", "zC", "yA"), ("zC", "yA", "yB")))


def coords(device):
    return tuple(int(v) for v in np.unravel_index(device, SIZES))


def ident(at):
    return int(np.ravel_multi_index(at, SIZES))


def flip(at, dim):
    y, zh, zl, x, c = at
    return {
        "yA": (y ^ 1, zh, zl, x, c),
        "yB": (3 - y, zh, zl, x, c),
        "zC": (y, zh ^ 1, zl ^ 1, x, c),
        "zD": (y, zh, zl ^ 1, x, c),
        "xA": (y, zh, zl, x ^ 1, c),
        "xB": (y, zh, zl, 3 - x, c),
        "core": (y, zh, zl, x, 1 - c),
    }[dim]


def blocks_of(device, stream):
    at = coords(device)
    core = at[4]
    base = at if (at[0] >> 1) == core else flip(at, "yB")
    out = []
    for j in range(32):
        owner = base
        for k, dim in enumerate(RS_A[core][stream] + RS_B[core][stream]):
            if (j >> (4 - k)) & 1:
                owner = flip(owner, dim)
        out.append(ident(owner) // 2)
    return out


def shards_of(device, stream):
    at = coords(device)
    out = []
    for j in range(8):
        holder = at
        for k, dim in enumerate(AG[at[4]][stream]):
            if (j >> k) & 1:
                holder = flip(holder, dim)
        out.append(holder[0] * 2 + holder[1])
    return out


def table():
    rows = []
    for device in range(128):
        other = device ^ 1
        first, second = blocks_of(device, 0), blocks_of(device, 1)
        row = blocks_of(other, 0) + first + second
        for base in (16, 0):
            groups = []
            for g in range(4):
                at = [first.index(v) for v in second[base + 4 * g : base + 4 * g + 4]]
                assert at[0] % 4 == 0 and at == list(range(at[0], at[0] + 4))
                groups.append(at[0] // 4)
            early = [max(g - 4, 0) for g in groups]
            late = [min(g, 3) for g in groups]
            row += [int(g >= 4) for g in groups]
            for g in range(1, 4):
                early[g] = early[g] if groups[g] >= 4 else early[g - 1]
                late[g] = late[g] if groups[g] < 4 else late[g - 1]
            row += early + late
        for gatherer in (device, other):
            core = gatherer % 2
            both = [shards_of(gatherer, stream) for stream in range(2)]
            row += [v * 2 + core for v in both[0]] + both[0] + both[1] + [core]
        rows.append(row)
    return np.array(rows, np.int32)


def move(value, dims_of_core):
    pairs = []
    for device in range(128):
        at = coords(device)
        pairs.append((device, ident(flip(at, dims_of_core[at[4]]))))
    return lax.ppermute(value, AXES, pairs)


def move_some(value, want_mine, dims):
    pairs = []
    for device in range(128):
        at = coords(device)
        if ((at[0] >> 1) == at[4]) == want_mine:
            to = at
            for dim in dims:
                to = flip(to, dim)
            pairs.append((device, ident(to)))
    return lax.ppermute(value, AXES, pairs)


VMEM = 56 * 1024 * 1024


def gather_body(idx_ref, *refs):
    for k in range(4):
        refs[4][0, :, k * BLK : (k + 1) * BLK] = refs[k][...]


def gather_blocks(idx, acts):
    tokens = acts.shape[0]
    groups = idx.shape[0] // 4
    specs = [pl.BlockSpec((tokens, BLK), functools.partial(lambda k, i, w: (0, w[4 * i + k]), k)) for k in range(4)]
    return pl.pallas_call(
        gather_body,
        grid_spec=pltpu.PrefetchScalarGridSpec(
            num_scalar_prefetch=1,
            grid=(groups,),
            in_specs=specs,
            out_specs=pl.BlockSpec((1, tokens, 4 * BLK), lambda i, w: (i, 0, 0)),
        ),
        out_shape=jax.ShapeDtypeStruct((groups, tokens, 4 * BLK), acts.dtype),
        compiler_params=pltpu.CompilerParams(vmem_limit_bytes=VMEM),
        cost_estimate=pl.CostEstimate(flops=0, bytes_accessed=1024, transcendentals=0),
    )(idx, *([acts] * 4))


def partial_body(low, high, norm, n_got, where_ref, *refs):
    own = jnp.concatenate([ref[...] for ref in refs[0:4]], axis=1)
    gots = refs[4 : 4 + n_got]
    kt_own, kt_got = refs[4 + n_got : 6 + n_got]
    out_ref = refs[-1]
    got = gots[0][0]
    if n_got == 2:
        step = pl.program_id(0)
        got = jnp.where(where_ref[4 * pl.num_programs(0) + step] == 1, got, gots[1][0])
    total = jnp.dot(kt_own[low:high, :], own, preferred_element_type=jnp.float32)
    total += jnp.dot(kt_got[low:high, :], got, preferred_element_type=jnp.float32)
    total = (total * norm).astype(jnp.bfloat16)
    for k in range(4):
        out_ref[k] = total[:, k * BLK : (k + 1) * BLK]


def partial_blocks(where, acts, gots, kt_own, kt_got, low, high, norm, after=()):
    tokens = acts.shape[0]
    groups = 4
    specs = [pl.BlockSpec((tokens, BLK), functools.partial(lambda k, i, w: (0, w[4 * i + k]), k)) for k in range(4)]
    if len(gots) == 1:
        specs += [pl.BlockSpec((1, tokens, 4 * BLK), lambda i, w: (i, 0, 0))]
    else:
        specs += [
            pl.BlockSpec((1, tokens, 4 * BLK), functools.partial(lambda k, i, w: (w[(5 + k) * groups + i], 0, 0), k))
            for k in range(2)
        ]
    specs += [pl.BlockSpec(kt_own.shape, lambda i, w: (0, 0))] * 2
    specs += [pl.BlockSpec(memory_space=pl.ANY)] * len(after)
    width = high - low
    return pl.pallas_call(
        functools.partial(partial_body, low, high, norm, len(gots)),
        grid_spec=pltpu.PrefetchScalarGridSpec(
            num_scalar_prefetch=1,
            grid=(groups,),
            in_specs=specs,
            out_specs=pl.BlockSpec((4, width, BLK), lambda i, w: (i, 0, 0)),
        ),
        out_shape=jax.ShapeDtypeStruct((4 * groups, width, BLK), jnp.bfloat16),
        compiler_params=pltpu.CompilerParams(vmem_limit_bytes=VMEM),
        cost_estimate=pl.CostEstimate(flops=0, bytes_accessed=1024, transcendentals=0),
    )(where, *([acts] * 4), *gots, kt_own, kt_got, *after)


def project_body(half, rest, n_last, sched_ref, kg_ref, *refs):
    pieces = refs[:4]
    out_ref, wbuf, sem_a, sem_b = refs[4 + n_last :]
    step = pl.program_id(0)

    def piece(stream, j):
        source = pieces[stream * 2 + j // 4].at[j % 4]
        rows = T1 if stream == 0 else rest
        first = sched_ref[8 + stream * 8 + j] * half + (0 if stream == 0 else T1)
        sem = (sem_a if stream == 0 else sem_b).at[j]
        return pltpu.make_async_copy(source, wbuf.at[pl.ds(pl.multiple_of(first, 16), rows), :], sem)

    @pl.when(step == 0)
    def _():
        for stream in (1, 0):
            for j in range(8):
                piece(stream, j).start()
        for j in range(8):
            piece(1, j).wait()

    for j in range(8):

        @pl.when(step == j)
        def _(j=j):
            piece(0, j).wait()

    start = pl.multiple_of(sched_ref[8 + step] * half, half)
    out_ref[...] = lax.dot_general(
        kg_ref[...], wbuf[pl.ds(start, half), :], (((1,), (1,)), ((), ())), preferred_element_type=jnp.float32
    ).astype(jnp.bfloat16)


def project(sched, key_grads, pieces, half, last=None):
    tokens, width = key_grads.shape
    rest = half - T1
    lasts = [] if last is None else [last]
    return pl.pallas_call(
        functools.partial(project_body, half, rest, len(lasts)),
        grid_spec=pltpu.PrefetchScalarGridSpec(
            num_scalar_prefetch=1,
            grid=(8,),
            in_specs=[pl.BlockSpec((tokens, width), lambda i, s: (0, 0))]
            + [pl.BlockSpec(memory_space=pl.ANY)] * (4 + len(lasts)),
            out_specs=pl.BlockSpec((tokens, half), lambda i, s: (0, s[i])),
            scratch_shapes=[
                pltpu.VMEM((8 * half, width), jnp.bfloat16),
                pltpu.SemaphoreType.DMA((8,)),
                pltpu.SemaphoreType.DMA((8,)),
            ],
        ),
        out_shape=jax.ShapeDtypeStruct((tokens, 16 * half), jnp.bfloat16),
        input_output_aliases={6: 0} if lasts else {},
        compiler_params=pltpu.CompilerParams(vmem_limit_bytes=VMEM),
        cost_estimate=pl.CostEstimate(flops=0, bytes_accessed=1024, transcendentals=0),
    )(sched, key_grads, *pieces, *lasts)


def add16(a, b):
    return (a.astype(jnp.float32) + b.astype(jnp.float32)).astype(jnp.bfloat16)


def shards(acts, key_grads, key_weight):
    tokens, model = acts.shape
    norm = float((tokens * 128) ** -0.5)
    device = lax.axis_index(AXES)
    core = device % 2
    y_hi = device // 64
    mine = core == y_hi
    row = lax.dynamic_index_in_dim(jnp.asarray(table()), device, 0, keepdims=False)

    half = key_weight.shape[0] // 2
    own_half = lax.dynamic_slice_in_dim(key_weight, core * half, half, axis=0)
    kt_own = key_grads.T
    kt_got = move(kt_own, ("core", "core"))
    early_sent, late_sent = gather_blocks(row[16:32], acts), gather_blocks(row[:16], acts)
    early, late = move(early_sent, ("core", "core")), move(late_sent, ("core", "core"))
    width = key_grads.shape[1]
    part = functools.partial(partial_blocks, acts=acts, kt_own=kt_own, kt_got=kt_got, norm=norm)
    first, second = row[32:64], row[64:96]
    part_second = part(jnp.concatenate([second[16:], row[96:108]]), gots=[early, late], low=S1, high=width)
    have = [own_half[None, :T1], own_half[None, T1:]]
    stages = []
    for stage in range(2):
        got = [move(have[k], (AG[0][k][stage], AG[1][k][stage])) for k in range(2)]
        if stage == 0:
            *got, late_sent = lax.optimization_barrier((*got, late_sent))
        else:
            *got, part_second = lax.optimization_barrier((*got, part_second))
        have = [jnp.concatenate([have[k], got[k]], axis=0) for k in range(2)]
        have = list(lax.optimization_barrier(tuple(have)))
        stages.append(have)
    got = [move(have[k], (AG[0][k][2], AG[1][k][2])) for k in range(2)]
    gathered = [have[0], got[0], have[1], got[1]]
    swapped = [move(g, ("core", "core")) for g in gathered]

    sends = [
        part(first[16:], gots=[early], low=0, high=S1, after=stages[0]),
        part_second,
    ]
    keeps = [
        part(first[:16], gots=[late], low=0, high=S1, after=stages[1]),
        part(jnp.concatenate([second[:16], row[108:120]]), gots=[early, late], low=S1, high=width),
    ]
    proj = project(row[120:145], key_grads, gathered, half)
    input_grads = project(row[145:170], key_grads, swapped, half, proj)
    before = [[], gathered, [proj], [input_grads], []]
    finals = []
    for stream in range(2):
        dims = [RS_A[k][stream] + RS_B[k][stream] for k in range(2)]
        send, keep = sends[stream], keeps[stream]
        for stage in range(5):
            got = move(send, (dims[0][stage], dims[1][stage]))
            if before[stage]:
                got, keep, *_ = lax.optimization_barrier((got, keep, *before[stage]))
            n = keep.shape[0] // 2
            if stage < 4:
                send, keep = add16(keep[n:], got[n:]), add16(keep[:n], got[:n])
            else:
                finals.append(keep[0].astype(jnp.float32) + got[0].astype(jnp.float32))

    total = jnp.concatenate(finals, axis=0).T
    rows = total.shape[0] // 2
    for_me = lax.dynamic_slice_in_dim(total, core * rows, rows, axis=0)
    for_other = lax.dynamic_slice_in_dim(total, (1 - core) * rows, rows, axis=0)
    for_me16, for_other16 = for_me.astype(jnp.bfloat16), for_other.astype(jnp.bfloat16)
    local = move_some(for_other, True, ("core",))
    same = move_some(for_me16, False, ("yB",))
    cross = move_some(for_other16, False, ("yB", "core"))
    weight_grads = jnp.where(mine, for_me, 0.0) + local + same.astype(jnp.float32) + cross.astype(jnp.float32)

    return input_grads, weight_grads


def solution(mesh):
    spec = P(AXES, None)
    return jax.shard_map(
        shards, mesh=mesh, in_specs=(spec, spec, P("intra", None)), out_specs=(spec, spec), check_vma=False
    )
```

```python
import functools

import jax
import jax.numpy as jnp
import numpy as np
from jax import lax
from jax.experimental import pallas as pl
from jax.experimental.pallas import tpu as pltpu
from jax.sharding import PartitionSpec as P

SIZES = (4, 2, 2, 4, 2)
AXES = ("intra", "inter")
S1 = 688
T1 = 336
BLK = 128

RS_A = ((("xA", "xB", "zD"), ("zD", "xA", "xB")), (("xB", "zD", "xA"), ("zD", "xA", "xB")))
RS_B = ((("zC", "yA"), ("zC", "yA")), (("zC", "yA"), ("zC", "yA")))
PROJECT = ((0, 1), (1, 1))
AG = ((("yA", "yB", "zC"), ("zC", "yA", "yB")), (("yB", "zC", "yA"), ("zC", "yA", "yB")))


def coords(device):
    return tuple(int(v) for v in np.unravel_index(device, SIZES))


def ident(at):
    return int(np.ravel_multi_index(at, SIZES))


def flip(at, dim):
    y, zh, zl, x, c = at
    return {
        "yA": (y ^ 1, zh, zl, x, c),
        "yB": (3 - y, zh, zl, x, c),
        "zC": (y, zh ^ 1, zl ^ 1, x, c),
        "zD": (y, zh, zl ^ 1, x, c),
        "xA": (y, zh, zl, x ^ 1, c),
        "xB": (y, zh, zl, 3 - x, c),
        "core": (y, zh, zl, x, 1 - c),
    }[dim]


def blocks_of(device, stream):
    at = coords(device)
    core = at[4]
    base = at if (at[0] >> 1) == core else flip(at, "yB")
    out = []
    for j in range(32):
        owner = base
        for k, dim in enumerate(RS_A[core][stream] + RS_B[core][stream]):
            if (j >> (4 - k)) & 1:
                owner = flip(owner, dim)
        out.append(ident(owner) // 2)
    return out


def shards_of(device, stream):
    at = coords(device)
    out = []
    for j in range(8):
        holder = at
        for k, dim in enumerate(AG[at[4]][stream]):
            if (j >> k) & 1:
                holder = flip(holder, dim)
        out.append(holder[0] * 2 + holder[1])
    return out


def table():
    rows = []
    for device in range(128):
        other = device ^ 1
        row = []
        for stream in range(2):
            order = blocks_of(device, stream)
            row += [order.index(block + 32 * (device % 2)) for block in range(32)]
        for gatherer in (device, other):
            core = gatherer % 2
            both = [shards_of(gatherer, stream) for stream in range(2)]
            row += [v * 2 + core for v in both[0]] + [both[1].index(v) for v in both[0]]
        rows.append(row)
    return np.array(rows, np.int32)


def move(value, dims_of_core):
    pairs = []
    for device in range(128):
        at = coords(device)
        pairs.append((device, ident(flip(at, dims_of_core[at[4]]))))
    return lax.ppermute(value, AXES, pairs)


def deliver(value, dims, k):
    pairs = []
    for device in range(128):
        at = coords(device)
        y_hi = at[0] >> 1
        to = at if y_hi == at[4] else flip(at, "yB")
        for dim in dims:
            to = flip(to, dim)
        pairs.append((device, ident((*to[:4], y_hi ^ k))))
    return lax.ppermute(value, AXES, pairs)


VMEM = 56 * 1024 * 1024


def front_body(core_ref, acts, weight, own_a, own_b, act_a, act_b, wbuf, abuf, sems):
    half = weight.shape[0] // 2
    part = act_a.shape[1]
    core = core_ref[0]
    rows = pl.multiple_of(core * half, half)
    columns = pl.multiple_of((1 - core) * 2 * part, part)
    loads = [pltpu.make_async_copy(weight.at[pl.ds(rows, half)], wbuf, sems.at[0])] + [
        pltpu.make_async_copy(acts.at[:, pl.ds(columns + k * part, part)], abuf.at[k], sems.at[1 + k]) for k in range(2)
    ]
    stores = [
        pltpu.make_async_copy(wbuf.at[pl.ds(0, T1)], own_a.at[0], sems.at[3]),
        pltpu.make_async_copy(wbuf.at[pl.ds(T1, half - T1)], own_b.at[0], sems.at[4]),
        pltpu.make_async_copy(abuf.at[0], act_a, sems.at[5]),
        pltpu.make_async_copy(abuf.at[1], act_b, sems.at[6]),
    ]
    for load in loads:
        load.start()
    loads[0].wait()
    stores[0].start()
    stores[1].start()
    for k in range(2):
        loads[1 + k].wait()
        stores[2 + k].start()
    for store in stores:
        store.wait()


def front(core, acts, weight):
    tokens, model = acts.shape
    rows, width = weight.shape
    half, part = rows // 2, model // 4
    shapes = [(1, T1, width), (1, half - T1, width), (tokens, part), (tokens, part)]
    return pl.pallas_call(
        front_body,
        in_specs=[pl.BlockSpec(memory_space=pltpu.SMEM)] + [pl.BlockSpec(memory_space=pl.ANY)] * 2,
        out_specs=[pl.BlockSpec(memory_space=pl.ANY)] * 4,
        scratch_shapes=[
            pltpu.VMEM((half, width), jnp.bfloat16),
            pltpu.VMEM((2, tokens, part), jnp.bfloat16),
            pltpu.SemaphoreType.DMA((7,)),
        ],
        out_shape=[jax.ShapeDtypeStruct(shape, jnp.bfloat16) for shape in shapes],
        compiler_params=pltpu.CompilerParams(vmem_limit_bytes=VMEM),
        cost_estimate=pl.CostEstimate(flops=0, bytes_accessed=1024, transcendentals=0),
    )(core, acts, weight)


CHUNK = 4 * BLK
TILE = 256


def partial_body(norm, n_chunks, where_ref, acts, got_a, got_b, kt_own, kt_got, *refs):
    outs, rhs, kt, outbuf, sem_in, sem_kt, sem_out = refs[:4], *refs[4:]
    tokens = acts.shape[0]
    n_blocks = 4 * n_chunks
    base = where_ref[2 * n_blocks] * (n_chunks * CHUNK)
    lows = (0, S1, kt.shape[0])

    def own_copy(g):
        start = pl.multiple_of(base + g * CHUNK, CHUNK)
        return pltpu.make_async_copy(acts.at[:, pl.ds(start, CHUNK)], rhs.at[g, pl.ds(0, tokens), :], sem_in.at[2 * g])

    def got_copy(g):
        source = got_a if g < n_chunks // 2 else got_b
        start = (g % (n_chunks // 2)) * CHUNK
        return pltpu.make_async_copy(
            source.at[:, pl.ds(start, CHUNK)], rhs.at[g, pl.ds(tokens, tokens), :], sem_in.at[2 * g + 1]
        )

    def kt_copy(which):
        return pltpu.make_async_copy((kt_own, kt_got)[which], kt.at[:, pl.ds(which * tokens, tokens)], sem_kt.at[which])

    def out_copy(block, stream, target):
        source = outbuf.at[block, pl.ds(lows[stream], lows[stream + 1] - lows[stream]), :]
        return pltpu.make_async_copy(source, target, sem_out.at[2 * block + stream])

    def load(g):
        own_copy(g).start()
        got_copy(g).start()

    kt_copy(0).start()
    kt_copy(1).start()
    for g in range(3):
        load(g)
    kt_copy(0).wait()
    kt_copy(1).wait()
    for g in range(n_chunks):
        own_copy(g).wait()
        got_copy(g).wait()
        if g + 3 < n_chunks:
            load(g + 3)
        for row in range(0, kt.shape[0], TILE):
            total = jnp.dot(kt[row : row + TILE, :], rhs[g], preferred_element_type=jnp.float32)
            total = (total * norm).astype(jnp.bfloat16)
            for k in range(4):
                outbuf[4 * g + k, row : row + TILE, :] = total[:, k * BLK : (k + 1) * BLK]
        for k in range(4):
            block = 4 * g + k
            for stream in range(2):
                place = where_ref[stream * n_blocks + block]

                @pl.when(place >= n_blocks // 2)
                def _(block=block, stream=stream, place=place):
                    out_copy(block, stream, outs[2 * stream].at[place - n_blocks // 2]).start()

                @pl.when(place < n_blocks // 2)
                def _(block=block, stream=stream, place=place):
                    out_copy(block, stream, outs[2 * stream + 1].at[place]).start()

    for block in range(n_blocks):
        for stream in range(2):
            out_copy(block, stream, outs[2 * stream].at[0]).wait()


def partial_blocks(where, acts, got_a, got_b, kt_own, kt_got, norm, before=()):
    tokens, model = acts.shape
    width = kt_own.shape[0]
    n_chunks = model // 2 // CHUNK
    widths = (S1, S1, width - S1, width - S1)
    n_before = len(before)

    def body(where_ref, *refs):
        partial_body(norm, n_chunks, where_ref, *refs[:5], *refs[5 + n_before :])

    return pl.pallas_call(
        body,
        in_specs=[pl.BlockSpec(memory_space=pltpu.SMEM)] + [pl.BlockSpec(memory_space=pl.ANY)] * (5 + n_before),
        out_specs=[pl.BlockSpec(memory_space=pl.ANY)] * 4,
        scratch_shapes=[
            pltpu.VMEM((n_chunks, 2 * tokens, CHUNK), jnp.bfloat16),
            pltpu.VMEM((width, 2 * tokens), jnp.bfloat16),
            pltpu.VMEM((4 * n_chunks, width, BLK), jnp.bfloat16),
            pltpu.SemaphoreType.DMA((2 * n_chunks,)),
            pltpu.SemaphoreType.DMA((2,)),
            pltpu.SemaphoreType.DMA((8 * n_chunks,)),
        ],
        out_shape=[jax.ShapeDtypeStruct((2 * n_chunks, w, BLK), jnp.bfloat16) for w in widths],
        compiler_params=pltpu.CompilerParams(vmem_limit_bytes=VMEM),
        cost_estimate=pl.CostEstimate(flops=0, bytes_accessed=1024, transcendentals=0),
    )(where, acts, got_a, got_b, kt_own, kt_got, *before)


def project_body(half, rest, n_last, sched_ref, kg_ref, *refs):
    pieces = refs[:4]
    out, wbuf, outbuf, sem_a, sem_b, sem_out = refs[4 + n_last :]

    def first(j):
        return pltpu.make_async_copy(pieces[j // 4].at[j % 4], wbuf.at[j, pl.ds(0, T1), :], sem_a.at[j])

    def second(j, source):
        return pltpu.make_async_copy(source, wbuf.at[j, pl.ds(T1, rest), :], sem_b.at[j])

    def load(j):
        first(j).start()
        place = sched_ref[8 + j]
        for which in range(2):

            @pl.when(place // 4 == which)
            def _(which=which):
                second(j, pieces[2 + which].at[place % 4]).start()

    def out_copy(j):
        start = pl.multiple_of(sched_ref[j] * half, half)
        return pltpu.make_async_copy(outbuf.at[j], out.at[:, pl.ds(start, half)], sem_out.at[j])

    for j in range(2):
        load(j)
    for j in range(8):
        first(j).wait()
        second(j, pieces[2].at[0]).wait()
        if j + 2 < 8:
            load(j + 2)
        for row in range(0, half, TILE):
            outbuf[j, :, row : row + TILE] = lax.dot_general(
                kg_ref[...], wbuf[j, row : row + TILE, :], (((1,), (1,)), ((), ())), preferred_element_type=jnp.float32
            ).astype(jnp.bfloat16)
        out_copy(j).start()
    for j in range(8):
        out_copy(j).wait()


def project(sched, kg, pieces, half, last=None):
    tokens, width = kg.shape
    rest = half - T1
    lasts = [] if last is None else [last]
    return pl.pallas_call(
        functools.partial(project_body, half, rest, len(lasts)),
        in_specs=[pl.BlockSpec(memory_space=pltpu.SMEM), pl.BlockSpec(memory_space=pltpu.VMEM)]
        + [pl.BlockSpec(memory_space=pl.ANY)] * (4 + len(lasts)),
        out_specs=pl.BlockSpec(memory_space=pl.ANY),
        scratch_shapes=[
            pltpu.VMEM((8, half, width), jnp.bfloat16),
            pltpu.VMEM((8, tokens, half), jnp.bfloat16),
            pltpu.SemaphoreType.DMA((8,)),
            pltpu.SemaphoreType.DMA((8,)),
            pltpu.SemaphoreType.DMA((8,)),
        ],
        out_shape=jax.ShapeDtypeStruct((tokens, 16 * half), jnp.bfloat16),
        input_output_aliases={6: 0} if lasts else {},
        compiler_params=pltpu.CompilerParams(vmem_limit_bytes=VMEM),
        cost_estimate=pl.CostEstimate(flops=16 * tokens * width * half, bytes_accessed=30 * 1024 * 1024, transcendentals=0),
    )(sched, kg, *pieces, *lasts)


def join_body(n_in, *refs):
    ins, outs, bufs, sems = refs[:n_in], refs[n_in : n_in + n_in // 2], refs[n_in + n_in // 2 : -1], refs[-1]

    def load(k):
        count = ins[k].shape[0]
        return pltpu.make_async_copy(ins[k], bufs[k // 2].at[pl.ds((k % 2) * count, count)], sems.at[k])

    def store(k):
        return pltpu.make_async_copy(bufs[k], outs[k], sems.at[n_in + k])

    for k in range(n_in):
        load(k).start()
    for k in range(n_in // 2):
        load(2 * k).wait()
        load(2 * k + 1).wait()
        store(k).start()
    for k in range(n_in // 2):
        store(k).wait()


def join(pairs):
    ins = [v for pair in pairs for v in pair]
    shapes = [(2 * a.shape[0], *a.shape[1:]) for a, _ in pairs]
    return list(
        pl.pallas_call(
            functools.partial(join_body, len(ins)),
            in_specs=[pl.BlockSpec(memory_space=pl.ANY)] * len(ins),
            out_specs=[pl.BlockSpec(memory_space=pl.ANY)] * len(pairs),
            scratch_shapes=[pltpu.VMEM(shape, jnp.bfloat16) for shape in shapes]
            + [pltpu.SemaphoreType.DMA((len(ins) + len(pairs),))],
            out_shape=[jax.ShapeDtypeStruct(shape, jnp.bfloat16) for shape in shapes],
            compiler_params=pltpu.CompilerParams(vmem_limit_bytes=VMEM),
            cost_estimate=pl.CostEstimate(flops=0, bytes_accessed=1024, transcendentals=0),
        )(*ins)
    )


def split_body(y_hi_ref, *refs):
    ins, outs, whole = refs[:4], refs[4:12], refs[12]
    for j in range(4):
        low = 0
        for stream in range(2):
            keep, got = ins[2 * stream], ins[2 * stream + 1]
            width = keep.shape[1]
            whole[low : low + width, :] = keep[j].astype(jnp.float32) + got[j].astype(jnp.float32)
            low += width
        turned = whole[...].T.astype(jnp.bfloat16)
        half = turned.shape[0] // 2
        for k in range(2):
            outs[2 * j + k][...] = jnp.where(y_hi_ref[0] == k, turned[:half], turned[half:])


def split_blocks(y_hi, streams):
    ins = [v for pair in streams for v in pair]
    width = sum(keep.shape[1] for keep, _ in streams)
    return pl.pallas_call(
        split_body,
        in_specs=[pl.BlockSpec(memory_space=pltpu.SMEM)] + [pl.BlockSpec(memory_space=pltpu.VMEM)] * 4,
        out_specs=[pl.BlockSpec(memory_space=pltpu.VMEM)] * 8,
        scratch_shapes=[pltpu.VMEM((width, BLK), jnp.float32)],
        out_shape=[jax.ShapeDtypeStruct((BLK // 2, width), jnp.bfloat16)] * 8,
        compiler_params=pltpu.CompilerParams(vmem_limit_bytes=VMEM),
        cost_estimate=pl.CostEstimate(flops=0, bytes_accessed=1024, transcendentals=0),
    )(y_hi, *ins)


def after(values, *before):
    return lax.optimization_barrier((*values, *before))[: len(values)]


def add16(a, b):
    return (a.astype(jnp.float32) + b.astype(jnp.float32)).astype(jnp.bfloat16)


def shards(acts, key_grads, key_weight):
    tokens, model = acts.shape
    norm = float((tokens * 128) ** -0.5)
    device = lax.axis_index(AXES)
    core = device % 2
    y_hi = device // 64
    row = lax.dynamic_index_in_dim(jnp.asarray(table()), device, 0, keepdims=False)

    pair = ("core", "core")
    half = key_weight.shape[0] // 2
    width = key_grads.shape[1]
    kt_own = key_grads.T
    *have, act_a, act_b = front(core[None].astype(jnp.int32), acts, key_weight)
    kt_got, got_a, got_b = move(kt_own, pair), move(act_a, pair), move(act_b, pair)
    for stage in range(2):
        got = [move(have[k], (AG[0][k][stage], AG[1][k][stage])) for k in range(2)]
        if stage == 1:
            got = after(got, sends[0], keeps[0])
        have = join(list(zip(have, got)))
        if stage == 0:
            where = jnp.concatenate([row[:64], core[None].astype(jnp.int32)])
            parts = partial_blocks(where, acts, got_a, got_b, kt_own, kt_got, norm, have)
            sends, keeps = [parts[0], parts[2]], [parts[1], parts[3]]
    got = [move(have[k], (AG[0][k][2], AG[1][k][2])) for k in range(2)]
    gathered = [have[0], got[0], have[1], got[1]]
    swapped = [move(g, pair) for g in gathered]

    last, held = [], ()
    done = have[0]
    input_grads = None
    for stage in range(3):
        for stream in range(2):
            got = move(sends[stream], (RS_A[0][stream][stage], RS_A[1][stream][stage]))
            got, keep = after((got, keeps[stream]), done, *(held if stream == 1 else ()))
            if stage == 2:
                last.append((keep, got))
                continue
            n = keep.shape[0] // 2
            done = sends[stream] = add16(keep[n:], got[n:])
            keeps[stream] = add16(keep[:n], got[:n])
            if (stage, stream) == PROJECT[0]:
                (sched,) = after((row[64:80],), done)
                input_grads = project(sched, key_grads, gathered, half)
                held = (input_grads,)
            if (stage, stream) == PROJECT[1]:
                (sched,) = after((row[80:96],), done)
                input_grads = project(sched, key_grads, swapped, half, input_grads)
                held = (input_grads,)

    pieces = split_blocks(y_hi[None].astype(jnp.int32), last)
    weight_grads = 0.0
    for j in range(4):
        dims = [dim for bit, dim in zip((2, 1), RS_B[0][0]) if j & bit]
        for k in range(2):
            weight_grads = weight_grads + deliver(pieces[2 * j + k], dims, k).astype(jnp.float32)
    return input_grads, weight_grads


def solution(mesh):
    spec = P(AXES, None)
    return jax.shard_map(
        shards, mesh=mesh, in_specs=(spec, spec, P("intra", None)), out_specs=(spec, spec), check_vma=False
    )
```

```python
import functools

import jax
import jax.numpy as jnp
import numpy as np
from jax import lax
from jax.experimental import pallas as pl
from jax.experimental.pallas import tpu as pltpu
from jax.sharding import PartitionSpec as P

SIZES = (4, 2, 2, 4, 2)
AXES = ("intra", "inter")
S1 = 688
T1 = 336
BLK = 128

RS_A = ((("xA", "xB", "zD"), ("zD", "xA", "xB")), (("xB", "zD", "xA"), ("zD", "xA", "xB")))
RS_B = ((("zC", "yA"), ("zC", "yA")), (("zC", "yA"), ("zC", "yA")))
PROJECT = ((0, 1), (1, 1))
AG = ((("yA", "yB", "zC"), ("zC", "yA", "yB")), (("yB", "zC", "yA"), ("zC", "yA", "yB")))


def coords(device):
    return tuple(int(v) for v in np.unravel_index(device, SIZES))


def ident(at):
    return int(np.ravel_multi_index(at, SIZES))


def flip(at, dim):
    y, zh, zl, x, c = at
    return {
        "yA": (y ^ 1, zh, zl, x, c),
        "yB": (3 - y, zh, zl, x, c),
        "zC": (y, zh ^ 1, zl ^ 1, x, c),
        "zD": (y, zh, zl ^ 1, x, c),
        "xA": (y, zh, zl, x ^ 1, c),
        "xB": (y, zh, zl, 3 - x, c),
        "core": (y, zh, zl, x, 1 - c),
    }[dim]


def blocks_of(device, stream):
    at = coords(device)
    core = at[4]
    base = at if (at[0] >> 1) == core else flip(at, "yB")
    out = []
    for j in range(32):
        owner = base
        for k, dim in enumerate(RS_A[core][stream] + RS_B[core][stream]):
            if (j >> (4 - k)) & 1:
                owner = flip(owner, dim)
        out.append(ident(owner) // 2)
    return out


def shards_of(device, stream):
    at = coords(device)
    out = []
    for j in range(8):
        holder = at
        for k, dim in enumerate(AG[at[4]][stream]):
            if (j >> k) & 1:
                holder = flip(holder, dim)
        out.append(holder[0] * 2 + holder[1])
    return out


def table():
    rows = []
    for device in range(128):
        other = device ^ 1
        row = []
        for stream in range(2):
            order = blocks_of(device, stream)
            row += [order.index(block + 32 * (device % 2)) for block in range(32)]
        for gatherer in (device, other):
            core = gatherer % 2
            both = [shards_of(gatherer, stream) for stream in range(2)]
            row += [v * 2 + core for v in both[0]] + [both[1].index(v) for v in both[0]]
        rows.append(row)
    return np.array(rows, np.int32)


def move(value, dims_of_core):
    pairs = []
    for device in range(128):
        at = coords(device)
        pairs.append((device, ident(flip(at, dims_of_core[at[4]]))))
    return lax.ppermute(value, AXES, pairs)


def deliver(value, dims):
    pairs = []
    for device in range(128):
        at = coords(device)
        to = at if (at[0] >> 1) == at[4] else flip(flip(at, "yB"), "core")
        for dim in dims:
            to = flip(to, dim)
        pairs.append((device, ident(to)))
    return lax.ppermute(value, AXES, pairs)


VMEM = 56 * 1024 * 1024


def front_body(core_ref, acts, weight, own_a, own_b, act_a, act_b, wbuf, abuf, sems):
    half = weight.shape[0] // 2
    part = act_a.shape[1]
    core = core_ref[0]
    rows = pl.multiple_of(core * half, half)
    columns = pl.multiple_of((1 - core) * 2 * part, part)
    loads = [pltpu.make_async_copy(weight.at[pl.ds(rows, half)], wbuf, sems.at[0])] + [
        pltpu.make_async_copy(acts.at[:, pl.ds(columns + k * part, part)], abuf.at[k], sems.at[1 + k]) for k in range(2)
    ]
    stores = [
        pltpu.make_async_copy(wbuf.at[pl.ds(0, T1)], own_a.at[0], sems.at[3]),
        pltpu.make_async_copy(wbuf.at[pl.ds(T1, half - T1)], own_b.at[0], sems.at[4]),
        pltpu.make_async_copy(abuf.at[0], act_a, sems.at[5]),
        pltpu.make_async_copy(abuf.at[1], act_b, sems.at[6]),
    ]
    for load in loads:
        load.start()
    loads[0].wait()
    stores[0].start()
    stores[1].start()
    for k in range(2):
        loads[1 + k].wait()
        stores[2 + k].start()
    for store in stores:
        store.wait()


def front(core, acts, weight):
    tokens, model = acts.shape
    rows, width = weight.shape
    half, part = rows // 2, model // 4
    shapes = [(1, T1, width), (1, half - T1, width), (tokens, part), (tokens, part)]
    return pl.pallas_call(
        front_body,
        in_specs=[pl.BlockSpec(memory_space=pltpu.SMEM)] + [pl.BlockSpec(memory_space=pl.ANY)] * 2,
        out_specs=[pl.BlockSpec(memory_space=pl.ANY)] * 4,
        scratch_shapes=[
            pltpu.VMEM((half, width), jnp.bfloat16),
            pltpu.VMEM((2, tokens, part), jnp.bfloat16),
            pltpu.SemaphoreType.DMA((7,)),
        ],
        out_shape=[jax.ShapeDtypeStruct(shape, jnp.bfloat16) for shape in shapes],
        compiler_params=pltpu.CompilerParams(vmem_limit_bytes=VMEM),
        cost_estimate=pl.CostEstimate(flops=0, bytes_accessed=1024, transcendentals=0),
    )(core, acts, weight)


CHUNK = 4 * BLK
TILE = 256


def partial_body(norm, n_chunks, where_ref, acts, got_a, got_b, kt_own, kt_got, *refs):
    outs, rhs, kt, outbuf, sem_in, sem_kt, sem_out = refs[:4], *refs[4:]
    tokens = acts.shape[0]
    n_blocks = 4 * n_chunks
    base = where_ref[2 * n_blocks] * (n_chunks * CHUNK)
    lows = (0, S1, kt.shape[0])

    def own_copy(g):
        start = pl.multiple_of(base + g * CHUNK, CHUNK)
        return pltpu.make_async_copy(acts.at[:, pl.ds(start, CHUNK)], rhs.at[g, pl.ds(0, tokens), :], sem_in.at[2 * g])

    def got_copy(g):
        source = got_a if g < n_chunks // 2 else got_b
        start = (g % (n_chunks // 2)) * CHUNK
        return pltpu.make_async_copy(
            source.at[:, pl.ds(start, CHUNK)], rhs.at[g, pl.ds(tokens, tokens), :], sem_in.at[2 * g + 1]
        )

    def kt_copy(which):
        return pltpu.make_async_copy((kt_own, kt_got)[which], kt.at[:, pl.ds(which * tokens, tokens)], sem_kt.at[which])

    def out_copy(block, stream, target):
        source = outbuf.at[block, pl.ds(lows[stream], lows[stream + 1] - lows[stream]), :]
        return pltpu.make_async_copy(source, target, sem_out.at[2 * block + stream])

    def load(g):
        own_copy(g).start()
        got_copy(g).start()

    kt_copy(0).start()
    kt_copy(1).start()
    for g in range(3):
        load(g)
    kt_copy(0).wait()
    kt_copy(1).wait()
    for g in range(n_chunks):
        own_copy(g).wait()
        got_copy(g).wait()
        if g + 3 < n_chunks:
            load(g + 3)
        for row in range(0, kt.shape[0], TILE):
            total = jnp.dot(kt[row : row + TILE, :], rhs[g], preferred_element_type=jnp.float32)
            total = (total * norm).astype(jnp.bfloat16)
            for k in range(4):
                outbuf[4 * g + k, row : row + TILE, :] = total[:, k * BLK : (k + 1) * BLK]
        for k in range(4):
            block = 4 * g + k
            for stream in range(2):
                place = where_ref[stream * n_blocks + block]

                @pl.when(place >= n_blocks // 2)
                def _(block=block, stream=stream, place=place):
                    out_copy(block, stream, outs[2 * stream].at[place - n_blocks // 2]).start()

                @pl.when(place < n_blocks // 2)
                def _(block=block, stream=stream, place=place):
                    out_copy(block, stream, outs[2 * stream + 1].at[place]).start()

    for block in range(n_blocks):
        for stream in range(2):
            out_copy(block, stream, outs[2 * stream].at[0]).wait()


def partial_blocks(where, acts, got_a, got_b, kt_own, kt_got, norm, before=()):
    tokens, model = acts.shape
    width = kt_own.shape[0]
    n_chunks = model // 2 // CHUNK
    widths = (S1, S1, width - S1, width - S1)
    n_before = len(before)

    def body(where_ref, *refs):
        partial_body(norm, n_chunks, where_ref, *refs[:5], *refs[5 + n_before :])

    return pl.pallas_call(
        body,
        in_specs=[pl.BlockSpec(memory_space=pltpu.SMEM)] + [pl.BlockSpec(memory_space=pl.ANY)] * (5 + n_before),
        out_specs=[pl.BlockSpec(memory_space=pl.ANY)] * 4,
        scratch_shapes=[
            pltpu.VMEM((n_chunks, 2 * tokens, CHUNK), jnp.bfloat16),
            pltpu.VMEM((width, 2 * tokens), jnp.bfloat16),
            pltpu.VMEM((4 * n_chunks, width, BLK), jnp.bfloat16),
            pltpu.SemaphoreType.DMA((2 * n_chunks,)),
            pltpu.SemaphoreType.DMA((2,)),
            pltpu.SemaphoreType.DMA((8 * n_chunks,)),
        ],
        out_shape=[jax.ShapeDtypeStruct((2 * n_chunks, w, BLK), jnp.bfloat16) for w in widths],
        compiler_params=pltpu.CompilerParams(vmem_limit_bytes=VMEM),
        cost_estimate=pl.CostEstimate(flops=0, bytes_accessed=1024, transcendentals=0),
    )(where, acts, got_a, got_b, kt_own, kt_got, *before)


def project_body(half, rest, n_last, sched_ref, kg_ref, *refs):
    pieces = refs[:4]
    out, wbuf, outbuf, sem_a, sem_b, sem_out = refs[4 + n_last :]

    def first(j):
        return pltpu.make_async_copy(pieces[j // 4].at[j % 4], wbuf.at[j, pl.ds(0, T1), :], sem_a.at[j])

    def second(j, source):
        return pltpu.make_async_copy(source, wbuf.at[j, pl.ds(T1, rest), :], sem_b.at[j])

    def load(j):
        first(j).start()
        place = sched_ref[8 + j]
        for which in range(2):

            @pl.when(place // 4 == which)
            def _(which=which):
                second(j, pieces[2 + which].at[place % 4]).start()

    def out_copy(j):
        start = pl.multiple_of(sched_ref[j] * half, half)
        return pltpu.make_async_copy(outbuf.at[j], out.at[:, pl.ds(start, half)], sem_out.at[j])

    for j in range(2):
        load(j)
    for j in range(8):
        first(j).wait()
        second(j, pieces[2].at[0]).wait()
        if j + 2 < 8:
            load(j + 2)
        for row in range(0, half, TILE):
            outbuf[j, :, row : row + TILE] = lax.dot_general(
                kg_ref[...], wbuf[j, row : row + TILE, :], (((1,), (1,)), ((), ())), preferred_element_type=jnp.float32
            ).astype(jnp.bfloat16)
        out_copy(j).start()
    for j in range(8):
        out_copy(j).wait()


def project(sched, kg, pieces, half, last=None):
    tokens, width = kg.shape
    rest = half - T1
    lasts = [] if last is None else [last]
    return pl.pallas_call(
        functools.partial(project_body, half, rest, len(lasts)),
        in_specs=[pl.BlockSpec(memory_space=pltpu.SMEM), pl.BlockSpec(memory_space=pltpu.VMEM)]
        + [pl.BlockSpec(memory_space=pl.ANY)] * (4 + len(lasts)),
        out_specs=pl.BlockSpec(memory_space=pl.ANY),
        scratch_shapes=[
            pltpu.VMEM((8, half, width), jnp.bfloat16),
            pltpu.VMEM((8, tokens, half), jnp.bfloat16),
            pltpu.SemaphoreType.DMA((8,)),
            pltpu.SemaphoreType.DMA((8,)),
            pltpu.SemaphoreType.DMA((8,)),
        ],
        out_shape=jax.ShapeDtypeStruct((tokens, 16 * half), jnp.bfloat16),
        input_output_aliases={6: 0} if lasts else {},
        compiler_params=pltpu.CompilerParams(vmem_limit_bytes=VMEM),
        cost_estimate=pl.CostEstimate(flops=16 * tokens * width * half, bytes_accessed=30 * 1024 * 1024, transcendentals=0),
    )(sched, kg, *pieces, *lasts)


def join_body(n_in, *refs):
    ins, outs, bufs, sems = refs[:n_in], refs[n_in : n_in + n_in // 2], refs[n_in + n_in // 2 : -1], refs[-1]

    def load(k):
        count = ins[k].shape[0]
        return pltpu.make_async_copy(ins[k], bufs[k // 2].at[pl.ds((k % 2) * count, count)], sems.at[k])

    def store(k):
        return pltpu.make_async_copy(bufs[k], outs[k], sems.at[n_in + k])

    for k in range(n_in):
        load(k).start()
    for k in range(n_in // 2):
        load(2 * k).wait()
        load(2 * k + 1).wait()
        store(k).start()
    for k in range(n_in // 2):
        store(k).wait()


def join(pairs):
    ins = [v for pair in pairs for v in pair]
    shapes = [(2 * a.shape[0], *a.shape[1:]) for a, _ in pairs]
    return list(
        pl.pallas_call(
            functools.partial(join_body, len(ins)),
            in_specs=[pl.BlockSpec(memory_space=pl.ANY)] * len(ins),
            out_specs=[pl.BlockSpec(memory_space=pl.ANY)] * len(pairs),
            scratch_shapes=[pltpu.VMEM(shape, jnp.bfloat16) for shape in shapes]
            + [pltpu.SemaphoreType.DMA((len(ins) + len(pairs),))],
            out_shape=[jax.ShapeDtypeStruct(shape, jnp.bfloat16) for shape in shapes],
            compiler_params=pltpu.CompilerParams(vmem_limit_bytes=VMEM),
            cost_estimate=pl.CostEstimate(flops=0, bytes_accessed=1024, transcendentals=0),
        )(*ins)
    )


def split_body(*refs):
    ins, outs, whole = refs[:4], refs[4:8], refs[8]
    for j in range(4):
        low = 0
        for stream in range(2):
            keep, got = ins[2 * stream], ins[2 * stream + 1]
            width = keep.shape[1]
            whole[low : low + width, :] = keep[j].astype(jnp.float32) + got[j].astype(jnp.float32)
            low += width
        outs[j][...] = whole[...].T.astype(jnp.bfloat16)


def split_blocks(streams):
    ins = [v for pair in streams for v in pair]
    width = sum(keep.shape[1] for keep, _ in streams)
    return pl.pallas_call(
        split_body,
        in_specs=[pl.BlockSpec(memory_space=pltpu.VMEM)] * 4,
        out_specs=[pl.BlockSpec(memory_space=pltpu.VMEM)] * 4,
        scratch_shapes=[pltpu.VMEM((width, BLK), jnp.float32)],
        out_shape=[jax.ShapeDtypeStruct((BLK, width), jnp.bfloat16)] * 4,
        compiler_params=pltpu.CompilerParams(vmem_limit_bytes=VMEM),
        cost_estimate=pl.CostEstimate(flops=0, bytes_accessed=1024, transcendentals=0),
    )(*ins)


def after(values, *before):
    return lax.optimization_barrier((*values, *before))[: len(values)]


def add16(a, b):
    return (a.astype(jnp.float32) + b.astype(jnp.float32)).astype(jnp.bfloat16)


def shards(acts, key_grads, key_weight):
    tokens, model = acts.shape
    norm = float((tokens * 128) ** -0.5)
    device = lax.axis_index(AXES)
    core = device % 2
    row = lax.dynamic_index_in_dim(jnp.asarray(table()), device, 0, keepdims=False)

    pair = ("core", "core")
    half = key_weight.shape[0] // 2
    width = key_grads.shape[1]
    kt_own = key_grads.T
    *have, act_a, act_b = front(core[None].astype(jnp.int32), acts, key_weight)
    kt_got, got_a, got_b = move(kt_own, pair), move(act_a, pair), move(act_b, pair)
    for stage in range(2):
        got = [move(have[k], (AG[0][k][stage], AG[1][k][stage])) for k in range(2)]
        if stage == 1:
            got = after(got, sends[0], keeps[0])
        have = join(list(zip(have, got)))
        if stage == 0:
            where = jnp.concatenate([row[:64], core[None].astype(jnp.int32)])
            parts = partial_blocks(where, acts, got_a, got_b, kt_own, kt_got, norm, have)
            sends, keeps = [parts[0], parts[2]], [parts[1], parts[3]]
    got = [move(have[k], (AG[0][k][2], AG[1][k][2])) for k in range(2)]
    gathered = [have[0], got[0], have[1], got[1]]
    swapped = [move(g, pair) for g in gathered]

    last, held = [], ()
    done = have[0]
    input_grads = None
    for stage in range(3):
        for stream in range(2):
            got = move(sends[stream], (RS_A[0][stream][stage], RS_A[1][stream][stage]))
            got, keep = after((got, keeps[stream]), done, *(held if stream == 1 else ()))
            if stage == 2:
                last.append((keep, got))
                continue
            n = keep.shape[0] // 2
            done = sends[stream] = add16(keep[n:], got[n:])
            keeps[stream] = add16(keep[:n], got[:n])
            if (stage, stream) == PROJECT[0]:
                (sched,) = after((row[64:80],), done)
                input_grads = project(sched, key_grads, gathered, half)
                held = (input_grads,)
            if (stage, stream) == PROJECT[1]:
                (sched,) = after((row[80:96],), done)
                input_grads = project(sched, key_grads, swapped, half, input_grads)
                held = (input_grads,)

    pieces = split_blocks(last)
    total = 0.0
    for j in range(4):
        dims = [dim for bit, dim in zip((2, 1), RS_B[0][0]) if j & bit]
        total = total + deliver(pieces[j], dims).astype(jnp.float32)
    rows = total.shape[0] // 2
    for_other = lax.dynamic_slice_in_dim(total, (1 - core) * rows, rows, axis=0)
    weight_grads = lax.dynamic_slice_in_dim(total, core * rows, rows, axis=0) + move(for_other, pair)
    return input_grads, weight_grads


def solution(mesh):
    spec = P(AXES, None)
    return jax.shard_map(
        shards, mesh=mesh, in_specs=(spec, spec, P("intra", None)), out_specs=(spec, spec), check_vma=False
    )
```

```python
import functools

import jax
import jax.numpy as jnp
import numpy as np
from jax import lax
from jax.experimental import pallas as pl
from jax.experimental.pallas import tpu as pltpu
from jax.sharding import PartitionSpec as P

SIZES = (4, 2, 2, 4, 2)
AXES = ("intra", "inter")
S1 = 688
T1 = 336
BLK = 128

RS_A = ((("xA", "xB", "zD"), ("zD", "xA", "xB")), (("xB", "zD", "xA"), ("zD", "xA", "xB")))
RS_B = ((("zC", "yA"), ("zC", "yA")), (("zC", "yA"), ("zC", "yA")))
LATE = (0, 0)
PROJECT = ((0, 1), (1, 1))
AG = ((("yA", "yB", "zC"), ("zC", "yA", "yB")), (("yB", "zC", "yA"), ("zC", "yA", "yB")))


def coords(device):
    return tuple(int(v) for v in np.unravel_index(device, SIZES))


def ident(at):
    return int(np.ravel_multi_index(at, SIZES))


def flip(at, dim):
    y, zh, zl, x, c = at
    return {
        "yA": (y ^ 1, zh, zl, x, c),
        "yB": (3 - y, zh, zl, x, c),
        "zC": (y, zh ^ 1, zl ^ 1, x, c),
        "zD": (y, zh, zl ^ 1, x, c),
        "xA": (y, zh, zl, x ^ 1, c),
        "xB": (y, zh, zl, 3 - x, c),
        "core": (y, zh, zl, x, 1 - c),
    }[dim]


def blocks_of(device, stream):
    at = coords(device)
    core = at[4]
    base = at if (at[0] >> 1) == core else flip(at, "yB")
    out = []
    for j in range(32):
        owner = base
        for k, dim in enumerate(RS_A[core][stream] + RS_B[core][stream]):
            if (j >> (4 - k)) & 1:
                owner = flip(owner, dim)
        out.append(ident(owner) // 2)
    return out


def shards_of(device, stream):
    at = coords(device)
    out = []
    for j in range(8):
        holder = at
        for k, dim in enumerate(AG[at[4]][stream]):
            if (j >> k) & 1:
                holder = flip(holder, dim)
        out.append(holder[0] * 2 + holder[1])
    return out


def table():
    rows = []
    for device in range(128):
        other = device ^ 1
        row = []
        for stream in range(2):
            order = blocks_of(device, stream)
            row += [order.index(block + 32 * (device % 2)) for block in range(32)]
        for gatherer in (device, other):
            core = gatherer % 2
            both = [shards_of(gatherer, stream) for stream in range(2)]
            row += [v * 2 + core for v in both[0]] + [both[1].index(v) for v in both[0]]
        rows.append(row)
    return np.array(rows, np.int32)


def move(value, dims_of_core):
    pairs = []
    for device in range(128):
        at = coords(device)
        pairs.append((device, ident(flip(at, dims_of_core[at[4]]))))
    return lax.ppermute(value, AXES, pairs)


def deliver(value, dims):
    pairs = []
    for device in range(128):
        at = coords(device)
        to = at if (at[0] >> 1) == at[4] else flip(flip(at, "yB"), "core")
        for dim in dims:
            to = flip(to, dim)
        pairs.append((device, ident(to)))
    return lax.ppermute(value, AXES, pairs)


VMEM = 56 * 1024 * 1024


def front_body(core_ref, acts, weight, own_a, own_b, act_a, act_b, wbuf, abuf, sems):
    half = weight.shape[0] // 2
    part = act_a.shape[1]
    core = core_ref[0]
    rows = pl.multiple_of(core * half, half)
    columns = pl.multiple_of((1 - core) * 2 * part, part)
    loads = [pltpu.make_async_copy(weight.at[pl.ds(rows, half)], wbuf, sems.at[0])] + [
        pltpu.make_async_copy(acts.at[:, pl.ds(columns + k * part, part)], abuf.at[k], sems.at[1 + k]) for k in range(2)
    ]
    stores = [
        pltpu.make_async_copy(wbuf.at[pl.ds(0, T1)], own_a.at[0], sems.at[3]),
        pltpu.make_async_copy(wbuf.at[pl.ds(T1, half - T1)], own_b.at[0], sems.at[4]),
        pltpu.make_async_copy(abuf.at[0], act_a, sems.at[5]),
        pltpu.make_async_copy(abuf.at[1], act_b, sems.at[6]),
    ]
    for load in loads:
        load.start()
    loads[0].wait()
    stores[0].start()
    stores[1].start()
    for k in range(2):
        loads[1 + k].wait()
        stores[2 + k].start()
    for store in stores:
        store.wait()


def front(core, acts, weight):
    tokens, model = acts.shape
    rows, width = weight.shape
    half, part = rows // 2, model // 4
    shapes = [(1, T1, width), (1, half - T1, width), (tokens, part), (tokens, part)]
    return pl.pallas_call(
        front_body,
        in_specs=[pl.BlockSpec(memory_space=pltpu.SMEM)] + [pl.BlockSpec(memory_space=pl.ANY)] * 2,
        out_specs=[pl.BlockSpec(memory_space=pl.ANY)] * 4,
        scratch_shapes=[
            pltpu.VMEM((half, width), jnp.bfloat16),
            pltpu.VMEM((2, tokens, part), jnp.bfloat16),
            pltpu.SemaphoreType.DMA((7,)),
        ],
        out_shape=[jax.ShapeDtypeStruct(shape, jnp.bfloat16) for shape in shapes],
        compiler_params=pltpu.CompilerParams(vmem_limit_bytes=VMEM),
        cost_estimate=pl.CostEstimate(flops=0, bytes_accessed=1024, transcendentals=0),
    )(core, acts, weight)


CHUNK = 4 * BLK
TILE = 256


def partial_body(norm, n_chunks, where_ref, acts, got_a, got_b, kt_own, kt_got, *refs):
    outs, rhs, kt, outbuf, sem_in, sem_kt, sem_out = refs[:4], *refs[4:]
    tokens = acts.shape[0]
    n_blocks = 4 * n_chunks
    base = where_ref[2 * n_blocks] * (n_chunks * CHUNK)
    lows = (0, S1, kt.shape[0])

    def own_copy(g):
        start = pl.multiple_of(base + g * CHUNK, CHUNK)
        return pltpu.make_async_copy(acts.at[:, pl.ds(start, CHUNK)], rhs.at[g, pl.ds(0, tokens), :], sem_in.at[2 * g])

    def got_copy(g):
        source = got_a if g < n_chunks // 2 else got_b
        start = (g % (n_chunks // 2)) * CHUNK
        return pltpu.make_async_copy(
            source.at[:, pl.ds(start, CHUNK)], rhs.at[g, pl.ds(tokens, tokens), :], sem_in.at[2 * g + 1]
        )

    def kt_copy(which):
        return pltpu.make_async_copy((kt_own, kt_got)[which], kt.at[:, pl.ds(which * tokens, tokens)], sem_kt.at[which])

    def out_copy(block, stream, target):
        source = outbuf.at[block, pl.ds(lows[stream], lows[stream + 1] - lows[stream]), :]
        return pltpu.make_async_copy(source, target, sem_out.at[2 * block + stream])

    def load(g):
        own_copy(g).start()
        got_copy(g).start()

    kt_copy(0).start()
    kt_copy(1).start()
    for g in range(3):
        load(g)
    kt_copy(0).wait()
    kt_copy(1).wait()
    for g in range(n_chunks):
        own_copy(g).wait()
        got_copy(g).wait()
        if g + 3 < n_chunks:
            load(g + 3)
        for row in range(0, kt.shape[0], TILE):
            total = jnp.dot(kt[row : row + TILE, :], rhs[g], preferred_element_type=jnp.float32)
            total = (total * norm).astype(jnp.bfloat16)
            for k in range(4):
                outbuf[4 * g + k, row : row + TILE, :] = total[:, k * BLK : (k + 1) * BLK]
        for k in range(4):
            block = 4 * g + k
            for stream in range(2):
                place = where_ref[stream * n_blocks + block]

                @pl.when(place >= n_blocks // 2)
                def _(block=block, stream=stream, place=place):
                    out_copy(block, stream, outs[2 * stream].at[place - n_blocks // 2]).start()

                @pl.when(place < n_blocks // 2)
                def _(block=block, stream=stream, place=place):
                    out_copy(block, stream, outs[2 * stream + 1].at[place]).start()

    for block in range(n_blocks):
        for stream in range(2):
            out_copy(block, stream, outs[2 * stream].at[0]).wait()


def partial_blocks(where, acts, got_a, got_b, kt_own, kt_got, norm, before=()):
    tokens, model = acts.shape
    width = kt_own.shape[0]
    n_chunks = model // 2 // CHUNK
    widths = (S1, S1, width - S1, width - S1)
    n_before = len(before)

    def body(where_ref, *refs):
        partial_body(norm, n_chunks, where_ref, *refs[:5], *refs[5 + n_before :])

    return pl.pallas_call(
        body,
        in_specs=[pl.BlockSpec(memory_space=pltpu.SMEM)] + [pl.BlockSpec(memory_space=pl.ANY)] * (5 + n_before),
        out_specs=[pl.BlockSpec(memory_space=pl.ANY)] * 4,
        scratch_shapes=[
            pltpu.VMEM((n_chunks, 2 * tokens, CHUNK), jnp.bfloat16),
            pltpu.VMEM((width, 2 * tokens), jnp.bfloat16),
            pltpu.VMEM((4 * n_chunks, width, BLK), jnp.bfloat16),
            pltpu.SemaphoreType.DMA((2 * n_chunks,)),
            pltpu.SemaphoreType.DMA((2,)),
            pltpu.SemaphoreType.DMA((8 * n_chunks,)),
        ],
        out_shape=[jax.ShapeDtypeStruct((2 * n_chunks, w, BLK), jnp.bfloat16) for w in widths],
        compiler_params=pltpu.CompilerParams(vmem_limit_bytes=VMEM),
        cost_estimate=pl.CostEstimate(flops=0, bytes_accessed=1024, transcendentals=0),
    )(where, acts, got_a, got_b, kt_own, kt_got, *before)


def project_body(half, rest, n_last, sched_ref, kg_ref, *refs):
    pieces = refs[:4]
    out, wbuf, outbuf, sem_a, sem_b, sem_out = refs[4 + n_last :]

    def first(j):
        return pltpu.make_async_copy(pieces[j // 4].at[j % 4], wbuf.at[j, pl.ds(0, T1), :], sem_a.at[j])

    def second(j, source):
        return pltpu.make_async_copy(source, wbuf.at[j, pl.ds(T1, rest), :], sem_b.at[j])

    def load(j):
        first(j).start()
        place = sched_ref[8 + j]
        for which in range(2):

            @pl.when(place // 4 == which)
            def _(which=which):
                second(j, pieces[2 + which].at[place % 4]).start()

    def out_copy(j):
        start = pl.multiple_of(sched_ref[j] * half, half)
        return pltpu.make_async_copy(outbuf.at[j], out.at[:, pl.ds(start, half)], sem_out.at[j])

    for j in range(2):
        load(j)
    for j in range(8):
        first(j).wait()
        second(j, pieces[2].at[0]).wait()
        if j + 2 < 8:
            load(j + 2)
        for row in range(0, half, TILE):
            outbuf[j, :, row : row + TILE] = lax.dot_general(
                kg_ref[...], wbuf[j, row : row + TILE, :], (((1,), (1,)), ((), ())), preferred_element_type=jnp.float32
            ).astype(jnp.bfloat16)
        out_copy(j).start()
    for j in range(8):
        out_copy(j).wait()


def project(sched, kg, pieces, half, last=None):
    tokens, width = kg.shape
    rest = half - T1
    lasts = [] if last is None else [last]
    return pl.pallas_call(
        functools.partial(project_body, half, rest, len(lasts)),
        in_specs=[pl.BlockSpec(memory_space=pltpu.SMEM), pl.BlockSpec(memory_space=pltpu.VMEM)]
        + [pl.BlockSpec(memory_space=pl.ANY)] * (4 + len(lasts)),
        out_specs=pl.BlockSpec(memory_space=pl.ANY),
        scratch_shapes=[
            pltpu.VMEM((8, half, width), jnp.bfloat16),
            pltpu.VMEM((8, tokens, half), jnp.bfloat16),
            pltpu.SemaphoreType.DMA((8,)),
            pltpu.SemaphoreType.DMA((8,)),
            pltpu.SemaphoreType.DMA((8,)),
        ],
        out_shape=jax.ShapeDtypeStruct((tokens, 16 * half), jnp.bfloat16),
        input_output_aliases={6: 0} if lasts else {},
        compiler_params=pltpu.CompilerParams(vmem_limit_bytes=VMEM),
        cost_estimate=pl.CostEstimate(flops=16 * tokens * width * half, bytes_accessed=30 * 1024 * 1024, transcendentals=0),
    )(sched, kg, *pieces, *lasts)


def join_body(n_in, *refs):
    ins, outs, bufs, sems = refs[:n_in], refs[n_in : n_in + n_in // 2], refs[n_in + n_in // 2 : -1], refs[-1]

    def load(k):
        count = ins[k].shape[0]
        return pltpu.make_async_copy(ins[k], bufs[k // 2].at[pl.ds((k % 2) * count, count)], sems.at[k])

    def store(k):
        return pltpu.make_async_copy(bufs[k], outs[k], sems.at[n_in + k])

    for k in range(n_in):
        load(k).start()
    for k in range(n_in // 2):
        load(2 * k).wait()
        load(2 * k + 1).wait()
        store(k).start()
    for k in range(n_in // 2):
        store(k).wait()


def join(pairs):
    ins = [v for pair in pairs for v in pair]
    shapes = [(2 * a.shape[0], *a.shape[1:]) for a, _ in pairs]
    return list(
        pl.pallas_call(
            functools.partial(join_body, len(ins)),
            in_specs=[pl.BlockSpec(memory_space=pl.ANY)] * len(ins),
            out_specs=[pl.BlockSpec(memory_space=pl.ANY)] * len(pairs),
            scratch_shapes=[pltpu.VMEM(shape, jnp.bfloat16) for shape in shapes]
            + [pltpu.SemaphoreType.DMA((len(ins) + len(pairs),))],
            out_shape=[jax.ShapeDtypeStruct(shape, jnp.bfloat16) for shape in shapes],
            compiler_params=pltpu.CompilerParams(vmem_limit_bytes=VMEM),
            cost_estimate=pl.CostEstimate(flops=0, bytes_accessed=1024, transcendentals=0),
        )(*ins)
    )


def split_body(*refs):
    ins, outs, whole = refs[:4], refs[4:8], refs[8]
    for j in range(4):
        low = 0
        for stream in range(2):
            keep, got = ins[2 * stream], ins[2 * stream + 1]
            width = keep.shape[1]
            whole[low : low + width, :] = keep[j].astype(jnp.float32) + got[j].astype(jnp.float32)
            low += width
        outs[j][...] = whole[...].T.astype(jnp.bfloat16)


def split_blocks(streams):
    ins = [v for pair in streams for v in pair]
    width = sum(keep.shape[1] for keep, _ in streams)
    return pl.pallas_call(
        split_body,
        in_specs=[pl.BlockSpec(memory_space=pltpu.VMEM)] * 4,
        out_specs=[pl.BlockSpec(memory_space=pltpu.VMEM)] * 4,
        scratch_shapes=[pltpu.VMEM((width, BLK), jnp.float32)],
        out_shape=[jax.ShapeDtypeStruct((BLK, width), jnp.bfloat16)] * 4,
        compiler_params=pltpu.CompilerParams(vmem_limit_bytes=VMEM),
        cost_estimate=pl.CostEstimate(flops=0, bytes_accessed=1024, transcendentals=0),
    )(*ins)


def after(values, *before):
    return lax.optimization_barrier((*values, *before))[: len(values)]


def add16(a, b):
    return (a.astype(jnp.float32) + b.astype(jnp.float32)).astype(jnp.bfloat16)


def shards(acts, key_grads, key_weight):
    tokens, model = acts.shape
    norm = float((tokens * 128) ** -0.5)
    device = lax.axis_index(AXES)
    core = device % 2
    row = lax.dynamic_index_in_dim(jnp.asarray(table()), device, 0, keepdims=False)

    pair = ("core", "core")
    half = key_weight.shape[0] // 2
    width = key_grads.shape[1]
    kt_own = key_grads.T
    *have, act_a, act_b = front(core[None].astype(jnp.int32), acts, key_weight)
    kt_got, got_a, got_b = move(kt_own, pair), move(act_a, pair), move(act_b, pair)
    for stage in range(2):
        got = [move(have[k], (AG[0][k][stage], AG[1][k][stage])) for k in range(2)]
        if stage == 1:
            got = after(got, sends[0], keeps[0])
        have = join(list(zip(have, got)))
        if stage == 0:
            where = jnp.concatenate([row[:64], core[None].astype(jnp.int32)])
            parts = partial_blocks(where, acts, got_a, got_b, kt_own, kt_got, norm, have)
            sends, keeps = [parts[0], parts[2]], [parts[1], parts[3]]
    got_last = got = [move(have[k], (AG[0][k][2], AG[1][k][2])) for k in range(2)]
    gathered = [have[0], got[0], have[1], got[1]]
    swapped = [move(have[0], pair), None, move(have[1], pair), None]

    last, held = [], (swapped[0],)
    done = have[0]
    input_grads = None
    for stage in range(3):
        for stream in range(2):
            got = move(sends[stream], (RS_A[0][stream][stage], RS_A[1][stream][stage]))
            got, keep = after((got, keeps[stream]), done, *(held if (stage, stream) != (0, 0) else ()))
            if stage == 2:
                last.append((keep, got))
                continue
            n = keep.shape[0] // 2
            done = sends[stream] = add16(keep[n:], got[n:])
            keeps[stream] = add16(keep[:n], got[:n])
            if (stage, stream) == LATE:
                swapped[1], swapped[3] = (move(v, pair) for v in after(got_last, done))
            if (stage, stream) == PROJECT[0]:
                (sched,) = after((row[64:80],), done)
                input_grads = project(sched, key_grads, gathered, half)
                held = (input_grads,)
            if (stage, stream) == PROJECT[1]:
                (sched,) = after((row[80:96],), done)
                input_grads = project(sched, key_grads, swapped, half, input_grads)
                held = (input_grads,)

    pieces = split_blocks(last)
    total = 0.0
    for j in range(4):
        dims = [dim for bit, dim in zip((2, 1), RS_B[0][0]) if j & bit]
        total = total + deliver(pieces[j], dims).astype(jnp.float32)
    rows = total.shape[0] // 2
    for_other = lax.dynamic_slice_in_dim(total, (1 - core) * rows, rows, axis=0)
    weight_grads = lax.dynamic_slice_in_dim(total, core * rows, rows, axis=0) + move(for_other, pair)
    return input_grads, weight_grads


def solution(mesh):
    spec = P(AXES, None)
    return jax.shard_map(
        shards, mesh=mesh, in_specs=(spec, spec, P("intra", None)), out_specs=(spec, spec), check_vma=False
    )
```

```python
import functools

import jax
import jax.numpy as jnp
import numpy as np
from jax import lax
from jax.experimental import pallas as pl
from jax.experimental.pallas import tpu as pltpu
from jax.sharding import PartitionSpec as P

SIZES = (4, 2, 2, 4, 2)
AXES = ("intra", "inter")
S1 = 720
T1 = 336
BLK = 128

RS_A = ((("xA", "xB", "zD"), ("zD", "xA", "xB")), (("xB", "zD", "xA"), ("zD", "xA", "xB")))
RS_B = ((("zC", "yA"), ("zC", "yA")), (("zC", "yA"), ("zC", "yA")))
LATE = (0, 0)
PROJECT = ((0, 1), (1, 1))
AG = ((("yA", "yB", "zC"), ("zC", "yA", "yB")), (("yB", "zC", "yA"), ("zC", "yA", "yB")))


def coords(device):
    return tuple(int(v) for v in np.unravel_index(device, SIZES))


def ident(at):
    return int(np.ravel_multi_index(at, SIZES))


def flip(at, dim):
    y, zh, zl, x, c = at
    return {
        "yA": (y ^ 1, zh, zl, x, c),
        "yB": (3 - y, zh, zl, x, c),
        "zC": (y, zh ^ 1, zl ^ 1, x, c),
        "zD": (y, zh, zl ^ 1, x, c),
        "xA": (y, zh, zl, x ^ 1, c),
        "xB": (y, zh, zl, 3 - x, c),
        "core": (y, zh, zl, x, 1 - c),
    }[dim]


def blocks_of(device, stream):
    at = coords(device)
    core = at[4]
    base = at if (at[0] >> 1) == core else flip(at, "yB")
    out = []
    for j in range(32):
        owner = base
        for k, dim in enumerate(RS_A[core][stream] + RS_B[core][stream]):
            if (j >> (4 - k)) & 1:
                owner = flip(owner, dim)
        out.append(ident(owner) // 2)
    return out


def shards_of(device, stream):
    at = coords(device)
    out = []
    for j in range(8):
        holder = at
        for k, dim in enumerate(AG[at[4]][stream]):
            if (j >> k) & 1:
                holder = flip(holder, dim)
        out.append(holder[0] * 2 + holder[1])
    return out


def table():
    rows = []
    for device in range(128):
        other = device ^ 1
        row = []
        for stream in range(2):
            order = blocks_of(device, stream)
            row += [order.index(block + 32 * (device % 2)) for block in range(32)]
        for gatherer in (device, other):
            core = gatherer % 2
            both = [shards_of(gatherer, stream) for stream in range(2)]
            row += [v * 2 + core for v in both[0]] + [both[1].index(v) for v in both[0]]
        rows.append(row)
    return np.array(rows, np.int32)


def move(value, dims_of_core):
    pairs = []
    for device in range(128):
        at = coords(device)
        pairs.append((device, ident(flip(at, dims_of_core[at[4]]))))
    return lax.ppermute(value, AXES, pairs)


def deliver(value, dims):
    pairs = []
    for device in range(128):
        at = coords(device)
        to = at if (at[0] >> 1) == at[4] else flip(flip(at, "yB"), "core")
        for dim in dims:
            to = flip(to, dim)
        pairs.append((device, ident(to)))
    return lax.ppermute(value, AXES, pairs)


VMEM = 56 * 1024 * 1024


def front_body(core_ref, acts, weight, own_a, own_b, act_a, act_b, wbuf, abuf, sems):
    half = weight.shape[0] // 2
    part = act_a.shape[1]
    core = core_ref[0]
    rows = pl.multiple_of(core * half, half)
    columns = pl.multiple_of((1 - core) * 2 * part, part)
    loads = [pltpu.make_async_copy(weight.at[pl.ds(rows, half)], wbuf, sems.at[0])] + [
        pltpu.make_async_copy(acts.at[:, pl.ds(columns + k * part, part)], abuf.at[k], sems.at[1 + k]) for k in range(2)
    ]
    stores = [
        pltpu.make_async_copy(wbuf.at[pl.ds(0, T1)], own_a.at[0], sems.at[3]),
        pltpu.make_async_copy(wbuf.at[pl.ds(T1, half - T1)], own_b.at[0], sems.at[4]),
        pltpu.make_async_copy(abuf.at[0], act_a, sems.at[5]),
        pltpu.make_async_copy(abuf.at[1], act_b, sems.at[6]),
    ]
    for load in loads:
        load.start()
    loads[0].wait()
    stores[0].start()
    stores[1].start()
    for k in range(2):
        loads[1 + k].wait()
        stores[2 + k].start()
    for store in stores:
        store.wait()


def front(core, acts, weight):
    tokens, model = acts.shape
    rows, width = weight.shape
    half, part = rows // 2, model // 4
    shapes = [(1, T1, width), (1, half - T1, width), (tokens, part), (tokens, part)]
    return pl.pallas_call(
        front_body,
        in_specs=[pl.BlockSpec(memory_space=pltpu.SMEM)] + [pl.BlockSpec(memory_space=pl.ANY)] * 2,
        out_specs=[pl.BlockSpec(memory_space=pl.ANY)] * 4,
        scratch_shapes=[
            pltpu.VMEM((half, width), jnp.bfloat16),
            pltpu.VMEM((2, tokens, part), jnp.bfloat16),
            pltpu.SemaphoreType.DMA((7,)),
        ],
        out_shape=[jax.ShapeDtypeStruct(shape, jnp.bfloat16) for shape in shapes],
        compiler_params=pltpu.CompilerParams(vmem_limit_bytes=VMEM),
        cost_estimate=pl.CostEstimate(flops=0, bytes_accessed=1024, transcendentals=0),
    )(core, acts, weight)


CHUNK = 4 * BLK
TILE = 256


def partial_body(norm, n_chunks, where_ref, acts, got_a, got_b, kt_own, kt_got, *refs):
    outs, rhs, kt, outbuf, sem_in, sem_kt, sem_out = refs[:4], *refs[4:]
    tokens = acts.shape[0]
    n_blocks = 4 * n_chunks
    base = where_ref[2 * n_blocks] * (n_chunks * CHUNK)
    lows = (0, S1, kt.shape[0])

    def own_copy(g):
        start = pl.multiple_of(base + g * CHUNK, CHUNK)
        return pltpu.make_async_copy(acts.at[:, pl.ds(start, CHUNK)], rhs.at[g, pl.ds(0, tokens), :], sem_in.at[2 * g])

    def got_copy(g):
        source = got_a if g < n_chunks // 2 else got_b
        start = (g % (n_chunks // 2)) * CHUNK
        return pltpu.make_async_copy(
            source.at[:, pl.ds(start, CHUNK)], rhs.at[g, pl.ds(tokens, tokens), :], sem_in.at[2 * g + 1]
        )

    def kt_copy(which):
        return pltpu.make_async_copy((kt_own, kt_got)[which], kt.at[:, pl.ds(which * tokens, tokens)], sem_kt.at[which])

    def out_copy(block, stream, target):
        source = outbuf.at[block, pl.ds(lows[stream], lows[stream + 1] - lows[stream]), :]
        return pltpu.make_async_copy(source, target, sem_out.at[2 * block + stream])

    def load(g):
        own_copy(g).start()
        got_copy(g).start()

    kt_copy(0).start()
    kt_copy(1).start()
    for g in range(3):
        load(g)
    kt_copy(0).wait()
    kt_copy(1).wait()
    for g in range(n_chunks):
        own_copy(g).wait()
        got_copy(g).wait()
        if g + 3 < n_chunks:
            load(g + 3)
        for row in range(0, kt.shape[0], TILE):
            total = jnp.dot(kt[row : row + TILE, :], rhs[g], preferred_element_type=jnp.float32)
            total = (total * norm).astype(jnp.bfloat16)
            for k in range(4):
                outbuf[4 * g + k, row : row + TILE, :] = total[:, k * BLK : (k + 1) * BLK]
        for k in range(4):
            block = 4 * g + k
            for stream in range(2):
                place = where_ref[stream * n_blocks + block]

                @pl.when(place >= n_blocks // 2)
                def _(block=block, stream=stream, place=place):
                    out_copy(block, stream, outs[2 * stream].at[place - n_blocks // 2]).start()

                @pl.when(place < n_blocks // 2)
                def _(block=block, stream=stream, place=place):
                    out_copy(block, stream, outs[2 * stream + 1].at[place]).start()

    for block in range(n_blocks):
        for stream in range(2):
            out_copy(block, stream, outs[2 * stream].at[0]).wait()


def partial_blocks(where, acts, got_a, got_b, kt_own, kt_got, norm, before=()):
    tokens, model = acts.shape
    width = kt_own.shape[0]
    n_chunks = model // 2 // CHUNK
    widths = (S1, S1, width - S1, width - S1)
    n_before = len(before)

    def body(where_ref, *refs):
        partial_body(norm, n_chunks, where_ref, *refs[:5], *refs[5 + n_before :])

    return pl.pallas_call(
        body,
        in_specs=[pl.BlockSpec(memory_space=pltpu.SMEM)] + [pl.BlockSpec(memory_space=pl.ANY)] * (5 + n_before),
        out_specs=[pl.BlockSpec(memory_space=pl.ANY)] * 4,
        scratch_shapes=[
            pltpu.VMEM((n_chunks, 2 * tokens, CHUNK), jnp.bfloat16),
            pltpu.VMEM((width, 2 * tokens), jnp.bfloat16),
            pltpu.VMEM((4 * n_chunks, width, BLK), jnp.bfloat16),
            pltpu.SemaphoreType.DMA((2 * n_chunks,)),
            pltpu.SemaphoreType.DMA((2,)),
            pltpu.SemaphoreType.DMA((8 * n_chunks,)),
        ],
        out_shape=[jax.ShapeDtypeStruct((2 * n_chunks, w, BLK), jnp.bfloat16) for w in widths],
        compiler_params=pltpu.CompilerParams(vmem_limit_bytes=VMEM),
        cost_estimate=pl.CostEstimate(flops=0, bytes_accessed=1024, transcendentals=0),
    )(where, acts, got_a, got_b, kt_own, kt_got, *before)


def project_body(half, rest, n_last, sched_ref, kg_ref, *refs):
    pieces = refs[:4]
    out, wbuf, outbuf, sem_a, sem_b, sem_out = refs[4 + n_last :]

    def first(j):
        return pltpu.make_async_copy(pieces[j // 4].at[j % 4], wbuf.at[j, pl.ds(0, T1), :], sem_a.at[j])

    def second(j, source):
        return pltpu.make_async_copy(source, wbuf.at[j, pl.ds(T1, rest), :], sem_b.at[j])

    def load(j):
        first(j).start()
        place = sched_ref[8 + j]
        for which in range(2):

            @pl.when(place // 4 == which)
            def _(which=which):
                second(j, pieces[2 + which].at[place % 4]).start()

    def out_copy(j):
        start = pl.multiple_of(sched_ref[j] * half, half)
        return pltpu.make_async_copy(outbuf.at[j], out.at[:, pl.ds(start, half)], sem_out.at[j])

    for j in range(2):
        load(j)
    for j in range(8):
        first(j).wait()
        second(j, pieces[2].at[0]).wait()
        if j + 2 < 8:
            load(j + 2)
        for row in range(0, half, TILE):
            outbuf[j, :, row : row + TILE] = lax.dot_general(
                kg_ref[...], wbuf[j, row : row + TILE, :], (((1,), (1,)), ((), ())), preferred_element_type=jnp.float32
            ).astype(jnp.bfloat16)
        out_copy(j).start()
    for j in range(8):
        out_copy(j).wait()


def project(sched, kg, pieces, half, last=None):
    tokens, width = kg.shape
    rest = half - T1
    lasts = [] if last is None else [last]
    return pl.pallas_call(
        functools.partial(project_body, half, rest, len(lasts)),
        in_specs=[pl.BlockSpec(memory_space=pltpu.SMEM), pl.BlockSpec(memory_space=pltpu.VMEM)]
        + [pl.BlockSpec(memory_space=pl.ANY)] * (4 + len(lasts)),
        out_specs=pl.BlockSpec(memory_space=pl.ANY),
        scratch_shapes=[
            pltpu.VMEM((8, half, width), jnp.bfloat16),
            pltpu.VMEM((8, tokens, half), jnp.bfloat16),
            pltpu.SemaphoreType.DMA((8,)),
            pltpu.SemaphoreType.DMA((8,)),
            pltpu.SemaphoreType.DMA((8,)),
        ],
        out_shape=jax.ShapeDtypeStruct((tokens, 16 * half), jnp.bfloat16),
        input_output_aliases={6: 0} if lasts else {},
        compiler_params=pltpu.CompilerParams(vmem_limit_bytes=VMEM),
        cost_estimate=pl.CostEstimate(flops=16 * tokens * width * half, bytes_accessed=30 * 1024 * 1024, transcendentals=0),
    )(sched, kg, *pieces, *lasts)


def join_body(n_in, *refs):
    ins, outs, bufs, sems = refs[:n_in], refs[n_in : n_in + n_in // 2], refs[n_in + n_in // 2 : -1], refs[-1]

    def load(k):
        count = ins[k].shape[0]
        return pltpu.make_async_copy(ins[k], bufs[k // 2].at[pl.ds((k % 2) * count, count)], sems.at[k])

    def store(k):
        return pltpu.make_async_copy(bufs[k], outs[k], sems.at[n_in + k])

    for k in range(n_in):
        load(k).start()
    for k in range(n_in // 2):
        load(2 * k).wait()
        load(2 * k + 1).wait()
        store(k).start()
    for k in range(n_in // 2):
        store(k).wait()


def join(pairs):
    ins = [v for pair in pairs for v in pair]
    shapes = [(2 * a.shape[0], *a.shape[1:]) for a, _ in pairs]
    return list(
        pl.pallas_call(
            functools.partial(join_body, len(ins)),
            in_specs=[pl.BlockSpec(memory_space=pl.ANY)] * len(ins),
            out_specs=[pl.BlockSpec(memory_space=pl.ANY)] * len(pairs),
            scratch_shapes=[pltpu.VMEM(shape, jnp.bfloat16) for shape in shapes]
            + [pltpu.SemaphoreType.DMA((len(ins) + len(pairs),))],
            out_shape=[jax.ShapeDtypeStruct(shape, jnp.bfloat16) for shape in shapes],
            compiler_params=pltpu.CompilerParams(vmem_limit_bytes=VMEM),
            cost_estimate=pl.CostEstimate(flops=0, bytes_accessed=1024, transcendentals=0),
        )(*ins)
    )


def split_body(*refs):
    ins, outs, whole = refs[:4], refs[4:8], refs[8]
    for j in range(4):
        low = 0
        for stream in range(2):
            keep, got = ins[2 * stream], ins[2 * stream + 1]
            width = keep.shape[1]
            whole[low : low + width, :] = keep[j].astype(jnp.float32) + got[j].astype(jnp.float32)
            low += width
        outs[j][...] = whole[...].T.astype(jnp.bfloat16)


def split_blocks(streams):
    ins = [v for pair in streams for v in pair]
    width = sum(keep.shape[1] for keep, _ in streams)
    return pl.pallas_call(
        split_body,
        in_specs=[pl.BlockSpec(memory_space=pltpu.VMEM)] * 4,
        out_specs=[pl.BlockSpec(memory_space=pltpu.VMEM)] * 4,
        scratch_shapes=[pltpu.VMEM((width, BLK), jnp.float32)],
        out_shape=[jax.ShapeDtypeStruct((BLK, width), jnp.bfloat16)] * 4,
        compiler_params=pltpu.CompilerParams(vmem_limit_bytes=VMEM),
        cost_estimate=pl.CostEstimate(flops=0, bytes_accessed=1024, transcendentals=0),
    )(*ins)


def after(values, *before):
    return lax.optimization_barrier((*values, *before))[: len(values)]


def add16(a, b):
    return (a.astype(jnp.float32) + b.astype(jnp.float32)).astype(jnp.bfloat16)


def shards(acts, key_grads, key_weight):
    tokens, model = acts.shape
    norm = float((tokens * 128) ** -0.5)
    device = lax.axis_index(AXES)
    core = device % 2
    row = lax.dynamic_index_in_dim(jnp.asarray(table()), device, 0, keepdims=False)

    pair = ("core", "core")
    half = key_weight.shape[0] // 2
    width = key_grads.shape[1]
    kt_own = key_grads.T
    *have, act_a, act_b = front(core[None].astype(jnp.int32), acts, key_weight)
    kt_got, got_a, got_b = move(kt_own, pair), move(act_a, pair), move(act_b, pair)
    for stage in range(2):
        got = [move(have[k], (AG[0][k][stage], AG[1][k][stage])) for k in range(2)]
        if stage == 1:
            got = after(got, sends[0], keeps[0])
        have = join(list(zip(have, got)))
        if stage == 0:
            where = jnp.concatenate([row[:64], core[None].astype(jnp.int32)])
            parts = partial_blocks(where, acts, got_a, got_b, kt_own, kt_got, norm, have)
            sends, keeps = [parts[0], parts[2]], [parts[1], parts[3]]
    got_last = got = [move(have[k], (AG[0][k][2], AG[1][k][2])) for k in range(2)]
    gathered = [have[0], got[0], have[1], got[1]]
    swapped = [move(have[0], pair), None, move(have[1], pair), None]

    last, held = [], (swapped[0],)
    done = have[0]
    input_grads = None
    for stage in range(3):
        for stream in range(2):
            got = move(sends[stream], (RS_A[0][stream][stage], RS_A[1][stream][stage]))
            got, keep = after((got, keeps[stream]), done, *(held if (stage, stream) != (0, 0) else ()))
            if stage == 2:
                last.append((keep, got))
                continue
            n = keep.shape[0] // 2
            done = sends[stream] = add16(keep[n:], got[n:])
            keeps[stream] = add16(keep[:n], got[:n])
            if (stage, stream) == LATE:
                swapped[1], swapped[3] = (move(v, pair) for v in after(got_last, done))
            if (stage, stream) == PROJECT[0]:
                (sched,) = after((row[64:80],), done)
                input_grads = project(sched, key_grads, gathered, half)
                held = (input_grads,)
            if (stage, stream) == PROJECT[1]:
                (sched,) = after((row[80:96],), done)
                input_grads = project(sched, key_grads, swapped, half, input_grads)
                held = (input_grads,)

    pieces = split_blocks(last)
    total = 0.0
    for j in range(4):
        dims = [dim for bit, dim in zip((2, 1), RS_B[0][0]) if j & bit]
        total = total + deliver(pieces[j], dims).astype(jnp.float32)
    rows = total.shape[0] // 2
    for_other = lax.dynamic_slice_in_dim(total, (1 - core) * rows, rows, axis=0)
    weight_grads = lax.dynamic_slice_in_dim(total, core * rows, rows, axis=0) + move(for_other, pair)
    return input_grads, weight_grads


def solution(mesh):
    spec = P(AXES, None)
    return jax.shard_map(
        shards, mesh=mesh, in_specs=(spec, spec, P("intra", None)), out_specs=(spec, spec), check_vma=False
    )
```
